128 devices in a mesh: section: 8 (over z, y_lo), ctx: 8 (over x, core), tp: 2 (over y_hi).
Axes of the slice: x: 4, y: 4 (y_hi: 2, y_lo: 2; y = y_hi * 2 + y_lo), z: 4, core: 2. Of those that a mesh axis runs over, the one named last changes fastest.
Arguments:
- queries: bfloat16 [8, 1024, 8192], P('section', 'ctx', 'tp'), may hold values from -6 to 6
- span_keys: bfloat16 [8, 1024, 512], P('section', ('ctx', 'tp')), may hold values from -6 to 6
- span_values: bfloat16 [8, 1024, 512], P('section', ('ctx', 'tp')), may hold values from -6 to 6
- prefix_keys: bfloat16 [8, 6144, 512], P('section', ('ctx', 'tp')), may hold values from -6 to 6
- prefix_values: bfloat16 [8, 6144, 512], P('section', ('ctx', 'tp')), may hold values from -6 to 6
- out_weight: bfloat16 [8, 8192, 8192], P('section', 'tp', 'ctx'), may hold values from -0.375 to 0.375
- residual: bfloat16 [8, 1024, 8192], P('section', 'tp', 'ctx'), may hold values from -6 to 6
- block_slot: int32 [48], replicated, may hold values from 0 to 47, each once
- span_index: int32 [8], P('section'), may hold values from 3 to 6
Outputs:
- handoff: bfloat16 [8, 1024, 8192], P('section', 'tp', 'ctx')
The draws below stay inside these ranges and needn't reach their ends.
Inputs may be any that keep to these rules, and one draw needn't show every extreme that they name: `block_slot`: each page number appears once.
All inputs are finite; a program needn't handle non-finite values.
Results may differ from the reference program's by a relative error of at most 0.015.
Values may be sent and summed in bfloat16 or wider, within the bound.
A program may use at most 128 MiB of HBM per device.

```python
import math
import jax
import jax.numpy as jnp
from jax import lax

QH = 64
KVH = 4
HD = 128
DW = 8192
BLK = 128
Q_DEV = 128
P_DEV = 384
SECTIONS = 8
SPAN = 1024
PREFIX = 6144
NBLK = 48
N_TP = 2


def draw_queries(key, part):
    key = jax.random.fold_in(key, 11)
    shape = (SECTIONS, SPAN, QH * HD)
    sample = jnp.clip(1.4 * jax.random.normal(key, shape, jnp.float32), -6.0, 6.0)
    return sample.astype(jnp.bfloat16)


def draw_span_keys(key, part):
    key = jax.random.fold_in(key, 12)
    shape = (SECTIONS, SPAN, KVH * HD)
    sample = jnp.clip(1.4 * jax.random.normal(key, shape, jnp.float32), -6.0, 6.0)
    return sample.astype(jnp.bfloat16)


def set_ends(drawn, stream_key, smallest, largest):
    dims = drawn.shape
    spot = [jax.random.randint(jax.random.fold_in(stream_key, axis), (), 0, dims[axis]) for axis in range(len(dims))]
    drawn = drawn.at[tuple(spot)].set(smallest)
    longest = dims.index(max(dims))
    spot[longest] = (spot[longest] + 1) % dims[longest]
    return drawn.at[tuple(spot)].set(largest)


def block_scale(stream_key, extent, cuts, smallest, high):
    loudness = 1.0
    for position, blocks in cuts:
        steps = jax.random.uniform(jax.random.fold_in(jax.random.fold_in(stream_key, 6), position), (blocks,), jnp.float32, smallest / len(cuts), high / len(cuts))
        loudness = loudness * jnp.repeat(jnp.exp(steps), extent[position] // blocks).reshape((-1,) + (1,) * (len(extent) - 1 - position))
    return loudness


def scatter_about(rng, extent, deviation, bound, cuts=(), held_as=jnp.bfloat16):
    result = deviation * jax.random.normal(rng, extent, jnp.float32)
    if cuts:
        result = result * block_scale(rng, extent, cuts, -0.22, 0.18)
    return jnp.clip(result, -bound, bound).astype(held_as)


def setup_inputs(seed: int = 0) -> dict:
    seeds = jax.random.split(jax.random.key(seed), 10)
    return {
        "queries": draw_queries(jax.random.fold_in(seeds[9], 71), 0),
        "span_keys": draw_span_keys(jax.random.fold_in(seeds[9], 71), 0),
        "span_values": scatter_about(seeds[2], (SECTIONS, SPAN, KVH * HD), 1.0, 6.0, ((0, 8), (1, 16))),
        "prefix_keys": scatter_about(seeds[3], (SECTIONS, PREFIX, KVH * HD), 1.4, 6.0, ((0, 8), (1, 16))),
        "prefix_values": scatter_about(seeds[4], (SECTIONS, PREFIX, KVH * HD), 1.0, 6.0, ((0, 8), (1, 16))),
        "out_weight": scatter_about(seeds[5], (SECTIONS, QH * HD, DW), (QH * HD // 32) ** -0.5, 0.375, ((0, 8), (1, 2), (2, 8))),
        "residual": scatter_about(seeds[6], (SECTIONS, SPAN, DW), 1.0, 6.0, ((0, 8), (1, 2), (2, 8))),
        "block_slot": jax.random.permutation(seeds[7], NBLK).astype(jnp.int32),
        "span_index": set_ends(jax.random.randint(seeds[8], (SECTIONS,), P_DEV * N_TP // Q_DEV // 2, P_DEV * N_TP // Q_DEV + 1), jax.random.fold_in(seeds[8], 1), P_DEV * N_TP // Q_DEV // 2, (P_DEV * N_TP // Q_DEV + 1) - 1).astype(jnp.int32),
    }


NEGATIVE = -1e+30

def section_layer(queries, key_rows, value_rows, visible, out_weight, residual):
    group_size = QH // KVH
    score_scale = 1.0 / math.sqrt(HD)

    def one_head(head_index):
        kv_head = head_index // group_size
        head_queries = lax.dynamic_slice_in_dim(queries, head_index * HD, HD, 1)
        head_keys = lax.dynamic_slice_in_dim(key_rows, kv_head * HD, HD, 1)
        head_values = lax.dynamic_slice_in_dim(value_rows, kv_head * HD, HD, 1)
        scores = jnp.dot(head_queries, head_keys.T, preferred_element_type=jnp.float32) * score_scale
        scores = jnp.where(visible, scores, NEGATIVE)
        row_max = lax.optimization_barrier(jnp.max(scores, axis=1, keepdims=True))
        weights = jnp.where(visible, jnp.exp(scores - row_max), 0.0)
        row_sum = lax.optimization_barrier(jnp.sum(weights, axis=1, keepdims=True))
        numerator = jnp.dot(weights.astype(jnp.bfloat16), head_values, preferred_element_type=jnp.float32)
        return (numerator / row_sum).astype(jnp.bfloat16)
    head_outputs = lax.map(one_head, jnp.arange(QH, dtype=jnp.int32))
    heads = jnp.transpose(head_outputs, (1, 0, 2)).reshape(SPAN, QH * HD)
    projected = jnp.dot(heads, out_weight, preferred_element_type=jnp.float32)
    return (residual.astype(jnp.float32) + projected).astype(jnp.bfloat16)

def reference(queries, span_keys, span_values, prefix_keys, prefix_values, out_weight, residual, block_slot, span_index):
    positions = jnp.arange(SPAN, dtype=jnp.int32)
    causal = positions[None, :] <= positions[:, None]
    layers = []
    for section_number in range(SECTIONS):
        page_ok = block_slot < span_index[section_number] * (SPAN // BLK)
        prefix_ok = jnp.repeat(page_ok, BLK)
        visible = jnp.concatenate([jnp.broadcast_to(prefix_ok[None, :], (SPAN, PREFIX)), causal], axis=1)
        key_rows = jnp.concatenate([prefix_keys[section_number], span_keys[section_number]], axis=0)
        value_rows = jnp.concatenate([prefix_values[section_number], span_values[section_number]], axis=0)
        layers.append(section_layer(queries[section_number], key_rows, value_rows, visible, out_weight[section_number], residual[section_number]))
    stacked = jnp.stack(layers, axis=0)
    return jnp.roll(stacked, 1, axis=0)
```

```python
import functools
import math

import jax
import jax.numpy as jnp
from jax import lax
from jax.experimental import pallas as pl
from jax.experimental.pallas import tpu as pltpu
from jax.sharding import PartitionSpec as P

MESH = pl.DeviceIdType.MESH
HD = 128
BLK = 128
QB = 1024
PRE = 384
SPN = 64
SLOT = 2 * PRE
SPAN = 1024
VR = 144
LOW = -1e30
SOURCES = ((0, 0), (1, 0), (3, 0), (0, 1), (1, 1), (3, 1), (2, 0), (2, 1))


def where_am_i():
    ctx = lax.axis_index("ctx")
    return lax.axis_index("section"), ctx // 2, lax.rem(ctx, 2), lax.axis_index("tp")


def pick(index, table):
    value = jnp.int32(table[-1])
    for position in range(len(table) - 1):
        value = jnp.where(index == position, jnp.int32(table[position]), value)
    return value


def attention_kernel(
    q_hbm, sk_hbm, sv_hbm, pk_hbm, pv_hbm, slot_ref, limit_ref, heads_ref,
    kv, q_raw, q_t, k_two, v_t, ks_two, vs_raw, vs_t, scores, span_scores, tri, block_max, row_max, acc,
    send_sem, recv_sem, fwd_send, fwd_recv, q_send, q_recv, local_sem,
):
    section, x, core, tp = where_am_i()
    swap_x = 3 - x

    def device(dx, dt):
        return (section, lax.rem(x + dx, 4) * 2 + core, lax.rem(tp + dt, 2))

    sibling = (section, x * 2 + 1 - core, tp)
    swap_device = (section, swap_x * 2 + core, tp)

    barrier = pltpu.get_barrier_semaphore()
    for dx, dt in SOURCES[1:]:
        pl.semaphore_signal(barrier, inc=1, device_id=device(dx, dt), device_id_type=MESH)
    pl.semaphore_signal(barrier, inc=1, device_id=sibling, device_id_type=MESH)

    def own_parts(head):
        cols = pl.ds(pl.multiple_of(head * HD, HD), HD)
        return (
            (pk_hbm.at[:, cols], 0, 0, PRE),
            (pv_hbm.at[:, cols], 1, 0, PRE),
            (sk_hbm.at[:, cols], 0, PRE, SPN),
            (sv_hbm.at[:, cols], 1, PRE, SPN),
        )

    group = x // 2
    locals_ = [
        pltpu.make_async_copy(src, kv.at[0, core, which, pl.ds(at, rows)], local_sem.at[number])
        for number, (src, which, at, rows) in enumerate(own_parts(tp * 2 + group))
    ]
    q_cols = pl.ds(pl.multiple_of(group * 2048, 2048), 2048)
    other_cols = pl.ds(pl.multiple_of((1 - group) * 2048, 2048), 2048)
    locals_.append(pltpu.make_async_copy(q_hbm.at[:, q_cols], q_raw.at[0], local_sem.at[4]))
    for copy in locals_:
        copy.start()

    pl.semaphore_wait(barrier, 8)

    swap = pltpu.make_async_remote_copy(
        src_ref=q_hbm.at[:, other_cols], dst_ref=q_raw.at[1], send_sem=q_send, recv_sem=q_recv,
        device_id=swap_device, device_id_type=MESH,
    )
    swap.start()
    sends = []
    for number, (dx, dt) in enumerate(SOURCES):
        if number == 0:
            continue
        index = SOURCES.index(((4 - dx) % 4, dt))
        target_x = lax.rem(x + dx, 4)
        head = lax.rem(tp + dt, 2) * 2 + target_x // 2
        for part, (src, which, at, rows) in enumerate(own_parts(head)):
            copy = pltpu.make_async_remote_copy(
                src_ref=src, dst_ref=kv.at[index, core, which, pl.ds(at, rows)],
                send_sem=send_sem.at[number, part], recv_sem=recv_sem.at[index],
                device_id=device(dx, dt), device_id_type=MESH,
            )
            copy.start()
            sends.append(copy)

    def forward_copy(slot):
        return pltpu.make_async_remote_copy(
            src_ref=kv.at[slot, core], dst_ref=kv.at[slot, core], send_sem=fwd_send.at[slot],
            recv_sem=fwd_recv.at[slot], device_id=sibling, device_id_type=MESH,
        )

    def arrived_sibling(slot):
        pltpu.make_async_remote_copy(
            src_ref=kv.at[slot, 1 - core], dst_ref=kv.at[slot, 1 - core], send_sem=fwd_send.at[slot],
            recv_sem=fwd_recv.at[slot], device_id=sibling, device_id_type=MESH,
        ).wait_recv()

    def forward(slot):
        pltpu.make_async_copy(kv.at[slot, core], kv.at[slot, core], recv_sem.at[slot]).wait()
        forward_copy(slot).start()

    def source(slot):
        dx = pick(slot, [s[0] for s in SOURCES])
        dt = pick(slot, [s[1] for s in SOURCES])
        return lax.rem(x + dx, 4), lax.rem(tp + dt, 2)

    def prepare(slot):
        arrived_sibling(slot)
        from_x, from_tp = source(slot)
        for c in range(2):
            keys = kv[slot, c, 0, :PRE]
            at = pl.ds(c * PRE, PRE)
            k_two[slot, at, :HD] = keys
            k_two[slot, at, HD:] = keys
            for page in range(PRE // BLK):
                v_t[slot, :HD, pl.ds(c * PRE + page * BLK, BLK)] = (
                    kv[slot, c, 1, pl.ds(page * BLK, BLK)].astype(jnp.float32).T.astype(jnp.bfloat16)
                )
            place = pl.ds(pl.multiple_of(((from_x * 2 + c) * 2 + from_tp) * SPN, SPN), SPN)
            span_keys = kv[slot, c, 0, PRE:]
            ks_two[place, :HD] = span_keys
            ks_two[place, HD:] = span_keys
            vs_raw[place] = kv[slot, c, 1, PRE:]

    def turn_queries(chunk):
        scale = math.log2(math.e) / math.sqrt(HD)

        @pl.loop(0, 16)
        def _(head):
            cols = pl.ds(pl.multiple_of(head * HD, HD), HD)
            turned = (q_raw[chunk, :, cols].astype(jnp.float32) * scale).T
            high = turned.astype(jnp.bfloat16)
            at = pl.ds(pl.multiple_of(chunk * 2048 + head * HD, HD), HD)
            q_t[:HD, at] = high
            q_t[HD:, at] = (turned - high.astype(jnp.float32)).astype(jnp.bfloat16)

    ones = jnp.ones((VR - HD, SLOT), jnp.bfloat16)
    for slot in range(8):
        v_t[slot, HD:] = ones
    vs_t[HD:] = jnp.ones((VR - HD, SPAN), jnp.bfloat16)
    key_at = lax.broadcasted_iota(jnp.int32, (BLK, QB), 0)
    row_at = lax.rem(lax.broadcasted_iota(jnp.int32, (BLK, QB), 1), BLK)
    tri[...] = jnp.where(key_at <= row_at, 0.0, LOW)
    row_max[...] = jnp.full(row_max.shape, LOW, jnp.float32)

    @pl.loop(0, 4)
    def _(q):
        acc[q] = jnp.zeros((VR, QB), jnp.float32)

    for copy in locals_[:4]:
        copy.wait()
    forward_copy(0).start()
    locals_[4].wait()
    turn_queries(0)
    prepare(0)
    forward(1)

    limit = limit_ref[0] * 8

    def visible(slot, page):
        from_x, from_tp = source(slot)
        c, inner = divmod(page, PRE // BLK)
        number = ((from_x * 2 + c) * 2 + from_tp) * (PRE // BLK) + inner
        return slot_ref[number] < limit

    def score(slot, q, buffer):
        cols = pl.ds(pl.multiple_of(q * QB, QB), QB)
        value = jnp.dot(k_two[slot], q_t[:, cols], preferred_element_type=jnp.float32)
        scores[buffer] = value
        largest = jnp.full((1, QB), LOW, jnp.float32)
        for page in range(SLOT // BLK):
            page_max = jnp.max(value[page * BLK : (page + 1) * BLK], axis=0, keepdims=True)
            largest = jnp.maximum(largest, jnp.where(visible(slot, page), page_max, LOW))
        block_max[buffer] = largest

    def update(q, largest, weights_of, values, blocks):
        before = row_max[q]
        now = jnp.maximum(before, largest)
        row_max[q] = now
        weights = jnp.concatenate([weights_of(block, now) for block in range(blocks)], axis=0)
        added = jnp.dot(values, weights, preferred_element_type=jnp.float32)
        acc[q] = acc[q] * jnp.exp2(before - now) + added

    def process(slot, q, buffer):
        def weights_of(page, now):
            shift = jnp.where(visible(slot, page), now, -LOW)
            return jnp.exp2(scores[buffer, page * BLK : (page + 1) * BLK] - shift).astype(jnp.bfloat16)

        update(q, block_max[buffer], weights_of, v_t[slot], SLOT // BLK)

    def span_step(q, ctx_of):
        cols = pl.ds(pl.multiple_of(q * QB, QB), QB)
        value = jnp.dot(ks_two[...], q_t[:, cols], preferred_element_type=jnp.float32)
        span_scores[...] = value
        mine = pl.ds(pl.multiple_of(ctx_of * BLK, BLK), BLK)
        span_scores[mine] = span_scores[mine] + tri[...]
        largest = jnp.full((1, QB), LOW, jnp.float32)
        for block in range(SPAN // BLK):
            top = jnp.max(span_scores[pl.ds(block * BLK, BLK)], axis=0, keepdims=True)
            largest = jnp.maximum(largest, jnp.where(block <= ctx_of, top, LOW))

        def weights_of(block, now):
            shift = jnp.where(block <= ctx_of, now, -LOW)
            return jnp.exp2(span_scores[pl.ds(block * BLK, BLK)] - shift).astype(jnp.bfloat16)

        update(q, largest, weights_of, vs_t[...], SPAN // BLK)

    def finish(chunk, half):
        q = chunk * 2 + half
        share = 1.0 / acc[q, HD : HD + 1]
        for head in range(8):
            at = slice(head * HD, (head + 1) * HD)
            block = acc[q, :HD, at] * share[:, at]
            heads_ref[chunk, :, pl.ds(half * QB + head * HD, HD)] = block.T.astype(jnp.bfloat16)

    first = group
    own_ctx = x * 2 + core
    swap_ctx = swap_x * 2 + core

    def chunk_of(phase):
        return jnp.where(phase == 0, 0, jnp.where(phase == 1, 1, jnp.where(phase == 2, first, 1 - first)))

    def slot_of(step):
        return lax.rem(step, 4) + 4 * (step // 8)

    score(0, 0, 0)

    @pl.loop(0, 16)
    def _(step):
        phase = step // 4
        slot = slot_of(step)
        chunk = chunk_of(phase)
        later = jnp.minimum(step + 1, 15)

        @pl.when(step < 2)
        def _():
            forward(step + 2)

        @pl.when((step >= 4) & (step < 8))
        def _():
            forward(step)

        @pl.when((step < 3) | ((step >= 7) & (step < 11)))
        def _():
            prepare(slot_of(later))

        @pl.when(step == 3)
        def _():
            swap.wait_recv()
            turn_queries(1)

        score(slot, chunk * 2 + 1, 1)
        process(slot, chunk * 2, 0)
        score(slot_of(later), chunk_of(later // 4) * 2, 0)
        process(slot, chunk * 2 + 1, 1)

        @pl.when(step == 11)
        def _():
            for block in range(SPAN // BLK):
                at = pl.ds(block * BLK, BLK)
                vs_t[:HD, at] = vs_raw[at].astype(jnp.float32).T.astype(jnp.bfloat16)

        @pl.when((step == 11) | (step == 15))
        def _():
            @pl.loop(0, 2)
            def _(half):
                span_step(chunk * 2 + half, jnp.where(chunk == 0, own_ctx, swap_ctx))

            for half in range(2):
                finish(chunk, half)

    for copy in sends:
        copy.wait_send()
    swap.wait_send()

    @pl.loop(0, 8)
    def _(slot):
        forward_copy(slot).wait_send()


def attention(queries, span_keys, span_values, prefix_keys, prefix_values, block_slot, span_index):
    any_spec = pl.BlockSpec(memory_space=pl.ANY)
    smem = pl.BlockSpec(memory_space=pltpu.SMEM)
    vmem = pl.BlockSpec(memory_space=pltpu.VMEM)
    dma = pltpu.SemaphoreType.DMA
    bf16, f32 = jnp.bfloat16, jnp.float32
    return pl.pallas_call(
        attention_kernel,
        out_shape=jax.ShapeDtypeStruct((2, BLK, 2048), bf16),
        in_specs=[any_spec] * 5 + [smem, smem],
        out_specs=vmem,
        scratch_shapes=[
            pltpu.VMEM((8, 2, 2, PRE + SPN, HD), bf16),
            pltpu.VMEM((2, BLK, 2048), bf16),
            pltpu.VMEM((2 * HD, 4 * QB), bf16),
            pltpu.VMEM((8, SLOT, 2 * HD), bf16),
            pltpu.VMEM((8, VR, SLOT), bf16),
            pltpu.VMEM((SPAN, 2 * HD), bf16),
            pltpu.VMEM((SPAN, HD), bf16),
            pltpu.VMEM((VR, SPAN), bf16),
            pltpu.VMEM((2, SLOT, QB), f32),
            pltpu.VMEM((SPAN, QB), f32),
            pltpu.VMEM((BLK, QB), f32),
            pltpu.VMEM((2, 1, QB), f32),
            pltpu.VMEM((4, 1, QB), f32),
            pltpu.VMEM((4, VR, QB), f32),
            dma((8, 4)), dma((8,)), dma((8,)), dma((8,)), dma(()), dma(()), dma((5,)),
        ],
        compiler_params=pltpu.CompilerParams(
            collective_id=0, has_side_effects=True, vmem_limit_bytes=56 << 20
        ),
        name="attention",
    )(queries, span_keys, span_values, prefix_keys, prefix_values, block_slot, span_index)


def per_device(
    queries, span_keys, span_values, prefix_keys, prefix_values, out_weight, residual, block_slot, span_index
):
    heads = attention(
        queries[0], span_keys[0], span_values[0], prefix_keys[0], prefix_values[0], block_slot, span_index
    )
    every = lax.all_gather(heads, "ctx", axis=0)
    rows = []
    for ctx in range(8):
        other = (3 - ctx // 2) * 2 + ctx % 2
        pair = (every[ctx, 0], every[other, 1])
        rows.append(jnp.concatenate(pair if ctx < 4 else pair[::-1], axis=1))
    partial = jnp.dot(jnp.concatenate(rows, axis=0), out_weight[0], preferred_element_type=jnp.float32)
    summed = lax.psum_scatter(partial.astype(jnp.bfloat16), "tp", scatter_dimension=0, tiled=True)
    layer = (residual[0].astype(jnp.float32) + summed.astype(jnp.float32)).astype(jnp.bfloat16)
    sections = lax.axis_size("section")
    return lax.ppermute(layer, "section", [(i, (i + 1) % sections) for i in range(sections)])[None]


def solution(mesh):
    in_specs = (
        P("section", "ctx", "tp"),
        P("section", ("ctx", "tp"), None),
        P("section", ("ctx", "tp"), None),
        P("section", ("ctx", "tp"), None),
        P("section", ("ctx", "tp"), None),
        P("section", "tp", "ctx"),
        P("section", "tp", "ctx"),
        P(),
        P("section"),
    )
    return jax.shard_map(
        per_device, mesh=mesh, in_specs=in_specs, out_specs=P("section", "tp", "ctx"), check_vma=False
    )
```

```python
import functools
import math

import jax
import jax.numpy as jnp
from jax import lax
from jax.experimental import pallas as pl
from jax.experimental.pallas import tpu as pltpu
from jax.sharding import PartitionSpec as P

MESH = pl.DeviceIdType.MESH
HD = 128
BLK = 128
QB = 1024
PRE = 384
SPN = 64
SLOT = 2 * PRE
SPAN = 1024
VR = 144
LOW = -1e30
FIRST_ROWS = (0, 2, 2, 0)
LAST_ROWS = (3, 1, 1, 3)
SOURCES = ((0, 0), (1, 0), (3, 0), (0, 1), (1, 1), (3, 1), (2, 0), (2, 1))


def where_am_i():
    ctx = lax.axis_index("ctx")
    return lax.axis_index("section"), ctx // 2, lax.rem(ctx, 2), lax.axis_index("tp")


def pick(index, table):
    value = jnp.int32(table[-1])
    for position in range(len(table) - 1):
        value = jnp.where(index == position, jnp.int32(table[position]), value)
    return value


def layer_kernel(
    q_hbm, sk_hbm, sv_hbm, pk_hbm, pv_hbm, w_hbm, res_hbm, slot_ref, limit_ref, out_ref,
    heads, weight, rest, total, part, got, kv, q_raw, q_t, k_two, v_t, ks_two, vs_raw, vs_t, scores, span_scores, tri, block_max, row_max, acc,
    send_sem, recv_sem, fwd_send, fwd_recv, q_send, q_recv, local_sem, g_send, g_recv, h_send, h_recv,
):
    section, x, core, tp = where_am_i()
    swap_x = 3 - x

    def device(dx, dt):
        return (section, lax.rem(x + dx, 4) * 2 + core, lax.rem(tp + dt, 2))

    sibling = (section, x * 2 + 1 - core, tp)
    swap_device = (section, swap_x * 2 + core, tp)

    next_section, last_section = lax.rem(section + 1, 8), lax.rem(section + 7, 8)
    ctx = x * 2 + core
    barrier = pltpu.get_barrier_semaphore()
    for dx, dt in SOURCES[1:]:
        pl.semaphore_signal(barrier, inc=1, device_id=device(dx, dt), device_id_type=MESH)
    pl.semaphore_signal(barrier, inc=1, device_id=sibling, device_id_type=MESH)
    for half in range(2):
        pl.semaphore_signal(barrier, inc=1, device_id=(last_section, ctx, half), device_id_type=MESH)

    def own_parts(head):
        cols = pl.ds(pl.multiple_of(head * HD, HD), HD)
        return (
            (pk_hbm.at[:, cols], 0, 0, PRE),
            (pv_hbm.at[:, cols], 1, 0, PRE),
            (sk_hbm.at[:, cols], 0, PRE, SPN),
            (sv_hbm.at[:, cols], 1, PRE, SPN),
        )

    group = x // 2
    locals_ = [
        pltpu.make_async_copy(src, kv.at[0, core, which, pl.ds(at, rows)], local_sem.at[number])
        for number, (src, which, at, rows) in enumerate(own_parts(tp * 2 + group))
    ]
    q_cols = pl.ds(pl.multiple_of(group * 2048, 2048), 2048)
    other_cols = pl.ds(pl.multiple_of((1 - group) * 2048, 2048), 2048)
    locals_.append(pltpu.make_async_copy(q_hbm.at[:, q_cols], q_raw.at[0], local_sem.at[4]))
    locals_.append(pltpu.make_async_copy(w_hbm, weight, local_sem.at[5]))
    locals_.append(pltpu.make_async_copy(res_hbm, rest, local_sem.at[6]))
    for copy in locals_:
        copy.start()

    pl.semaphore_wait(barrier, 10)

    swap = pltpu.make_async_remote_copy(
        src_ref=q_hbm.at[:, other_cols], dst_ref=q_raw.at[1], send_sem=q_send, recv_sem=q_recv,
        device_id=swap_device, device_id_type=MESH,
    )
    swap.start()
    sends = []
    for number, (dx, dt) in enumerate(SOURCES):
        if number == 0:
            continue
        index = SOURCES.index(((4 - dx) % 4, dt))
        target_x = lax.rem(x + dx, 4)
        head = lax.rem(tp + dt, 2) * 2 + target_x // 2
        for piece, (src, which, at, rows) in enumerate(own_parts(head)):
            copy = pltpu.make_async_remote_copy(
                src_ref=src, dst_ref=kv.at[index, core, which, pl.ds(at, rows)],
                send_sem=send_sem.at[number, piece], recv_sem=recv_sem.at[index],
                device_id=device(dx, dt), device_id_type=MESH,
            )
            copy.start()
            sends.append(copy)

    def forward_copy(slot):
        return pltpu.make_async_remote_copy(
            src_ref=kv.at[slot, core], dst_ref=kv.at[slot, core], send_sem=fwd_send.at[slot],
            recv_sem=fwd_recv.at[slot], device_id=sibling, device_id_type=MESH,
        )

    def arrived_sibling(slot):
        pltpu.make_async_remote_copy(
            src_ref=kv.at[slot, 1 - core], dst_ref=kv.at[slot, 1 - core], send_sem=fwd_send.at[slot],
            recv_sem=fwd_recv.at[slot], device_id=sibling, device_id_type=MESH,
        ).wait_recv()

    def forward(slot):
        pltpu.make_async_copy(kv.at[slot, core], kv.at[slot, core], recv_sem.at[slot]).wait()
        forward_copy(slot).start()

    def source(slot):
        dx = pick(slot, [s[0] for s in SOURCES])
        dt = pick(slot, [s[1] for s in SOURCES])
        return lax.rem(x + dx, 4), lax.rem(tp + dt, 2)

    def prepare(slot):
        arrived_sibling(slot)
        from_x, from_tp = source(slot)
        for c in range(2):
            keys = kv[slot, c, 0, :PRE]
            at = pl.ds(c * PRE, PRE)
            k_two[slot, at, :HD] = keys
            k_two[slot, at, HD:] = keys
            for page in range(PRE // BLK):
                v_t[slot, :HD, pl.ds(c * PRE + page * BLK, BLK)] = (
                    kv[slot, c, 1, pl.ds(page * BLK, BLK)].astype(jnp.float32).T.astype(jnp.bfloat16)
                )
            place = pl.ds(pl.multiple_of(((from_x * 2 + c) * 2 + from_tp) * SPN, SPN), SPN)
            span_keys = kv[slot, c, 0, PRE:]
            ks_two[place, :HD] = span_keys
            ks_two[place, HD:] = span_keys
            vs_raw[place] = kv[slot, c, 1, PRE:]

    def turn_queries(chunk):
        scale = math.log2(math.e) / math.sqrt(HD)

        @pl.loop(0, 16)
        def _(head):
            cols = pl.ds(pl.multiple_of(head * HD, HD), HD)
            turned = (q_raw[chunk, :, cols].astype(jnp.float32) * scale).T
            high = turned.astype(jnp.bfloat16)
            at = pl.ds(pl.multiple_of(chunk * 2048 + head * HD, HD), HD)
            q_t[:HD, at] = high
            q_t[HD:, at] = (turned - high.astype(jnp.float32)).astype(jnp.bfloat16)

    ones = jnp.ones((VR - HD, SLOT), jnp.bfloat16)
    for slot in range(8):
        v_t[slot, HD:] = ones
    vs_t[HD:] = jnp.ones((VR - HD, SPAN), jnp.bfloat16)
    key_at = lax.broadcasted_iota(jnp.int32, (BLK, QB), 0)
    row_at = lax.rem(lax.broadcasted_iota(jnp.int32, (BLK, QB), 1), BLK)
    tri[...] = jnp.where(key_at <= row_at, 0.0, LOW)
    row_max[...] = jnp.full(row_max.shape, LOW, jnp.float32)

    @pl.loop(0, 4)
    def _(q):
        acc[q] = jnp.zeros((VR, QB), jnp.float32)

    for copy in locals_[:4]:
        copy.wait()
    forward_copy(0).start()
    locals_[4].wait()
    turn_queries(0)
    prepare(0)
    forward(1)

    limit = limit_ref[0] * 8

    def visible(slot, page):
        from_x, from_tp = source(slot)
        c, inner = divmod(page, PRE // BLK)
        number = ((from_x * 2 + c) * 2 + from_tp) * (PRE // BLK) + inner
        return slot_ref[number] < limit

    def score(slot, q, buffer):
        cols = pl.ds(pl.multiple_of(q * QB, QB), QB)
        value = jnp.dot(k_two[slot], q_t[:, cols], preferred_element_type=jnp.float32)
        scores[buffer] = value
        largest = jnp.full((1, QB), LOW, jnp.float32)
        for page in range(SLOT // BLK):
            page_max = jnp.max(value[page * BLK : (page + 1) * BLK], axis=0, keepdims=True)
            largest = jnp.maximum(largest, jnp.where(visible(slot, page), page_max, LOW))
        block_max[buffer] = largest

    def update(q, largest, weights_of, values, blocks):
        before = row_max[q]
        now = jnp.maximum(before, largest)
        row_max[q] = now
        weights = jnp.concatenate([weights_of(block, now) for block in range(blocks)], axis=0)
        added = jnp.dot(values, weights, preferred_element_type=jnp.float32)
        acc[q] = acc[q] * jnp.exp2(before - now) + added

    def process(slot, q, buffer):
        def weights_of(page, now):
            shift = jnp.where(visible(slot, page), now, -LOW)
            return jnp.exp2(scores[buffer, page * BLK : (page + 1) * BLK] - shift).astype(jnp.bfloat16)

        update(q, block_max[buffer], weights_of, v_t[slot], SLOT // BLK)

    def span_step(q, ctx_of):
        cols = pl.ds(pl.multiple_of(q * QB, QB), QB)
        value = jnp.dot(ks_two[...], q_t[:, cols], preferred_element_type=jnp.float32)
        span_scores[...] = value
        mine = pl.ds(pl.multiple_of(ctx_of * BLK, BLK), BLK)
        span_scores[mine] = span_scores[mine] + tri[...]
        largest = jnp.full((1, QB), LOW, jnp.float32)
        for block in range(SPAN // BLK):
            top = jnp.max(span_scores[pl.ds(block * BLK, BLK)], axis=0, keepdims=True)
            largest = jnp.maximum(largest, jnp.where(block <= ctx_of, top, LOW))

        def weights_of(block, now):
            shift = jnp.where(block <= ctx_of, now, -LOW)
            return jnp.exp2(span_scores[pl.ds(block * BLK, BLK)] - shift).astype(jnp.bfloat16)

        update(q, largest, weights_of, vs_t[...], SPAN // BLK)

    def rows_of(chip, turn):
        return jnp.where(turn == 0, pick(chip, FIRST_ROWS), pick(chip, LAST_ROWS))

    def place(dx, turn, half, c):
        chip = lax.rem(x + dx, 4)
        return heads.at[rows_of(chip, turn), chip // 2, half, c]

    right, left = device(1, 0), device(3, 0)

    def moved(kind, turn, half):
        top, bottom = pl.ds(0, BLK // 2), pl.ds(BLK // 2, BLK // 2)
        if kind == 0:
            src, to, dst = place(0, turn, half, core), right, place(3, turn, half, core)
        elif kind == 1:
            src, to, dst = place(0, turn, half, core), left, place(1, turn, half, core)
        elif kind == 2:
            src, to, dst = place(3, turn, half, core).at[top], right, place(2, turn, half, core).at[top]
        elif kind == 3:
            src, to, dst = place(1, turn, half, core).at[bottom], left, place(2, turn, half, core).at[bottom]
        else:
            dx = (0, 3, 1, 2)[kind - 4]
            src, to, dst = place(dx, turn, half, core), sibling, place(dx, turn, half, 1 - core)
        piece = turn * 2 + half
        sems = (g_send.at[piece, kind], g_recv.at[piece, kind])
        make = functools.partial(
            pltpu.make_async_remote_copy, send_sem=sems[0], recv_sem=sems[1], device_id=to, device_id_type=MESH
        )
        return make(src_ref=src, dst_ref=src), make(src_ref=dst, dst_ref=dst)

    def send(kind, turn, half):
        moved(kind, turn, half)[0].start()

    def arrived(kind, turn, half):
        moved(kind, turn, half)[1].wait_recv()

    def finish(chunk, half, turn):
        q = chunk * 2 + half
        share = 1.0 / acc[q, HD : HD + 1]
        mine = place(0, turn, half, core)
        for head in range(8):
            at = slice(head * HD, (head + 1) * HD)
            block = acc[q, :HD, at] * share[:, at]
            mine[:, pl.ds(head * HD, HD)] = block.T.astype(jnp.bfloat16)
        for kind in (0, 1, 4):
            send(kind, turn, half)

    def pass_on(turn, half):
        arrived(0, turn, half)
        send(2, turn, half)
        send(5, turn, half)
        arrived(1, turn, half)
        send(3, turn, half)
        send(6, turn, half)

    def pass_far(turn, half):
        arrived(2, turn, half)
        arrived(3, turn, half)
        send(7, turn, half)

    def project(rows, kv_head, second):
        tile = 256
        half_at = rows // 2
        inside = pl.ds(pl.multiple_of(lax.rem(rows, 2) * 256, 256), 256)

        @pl.loop(0, 1024 // tile)
        def _(number):
            cols = pl.ds(pl.multiple_of(number * tile, tile), tile)
            value = jnp.zeros((256, tile), jnp.float32)
            for half in range(2):
                depth = pl.ds(pl.multiple_of(kv_head * 2048 + half * 1024, 1024), 1024)
                value += jnp.dot(
                    heads[rows, kv_head, half].reshape(256, 1024), weight[depth, cols],
                    preferred_element_type=jnp.float32,
                )
            if second:
                extra = jnp.where(half_at == tp, rest[inside, cols].astype(jnp.float32), 0.0)
                part[rows, :, cols] = (total[:, cols] + value + extra).astype(jnp.bfloat16)
            else:
                total[:, cols] = value

    def hand_on(rows):
        return pltpu.make_async_remote_copy(
            src_ref=part.at[rows], dst_ref=got.at[tp, lax.rem(rows, 2)], send_sem=h_send.at[rows],
            recv_sem=h_recv.at[tp, lax.rem(rows, 2)], device_id=(next_section, ctx, rows // 2), device_id_type=MESH,
        )

    def handed(from_tp, turn):
        ref = got.at[from_tp, turn]
        pltpu.make_async_remote_copy(
            src_ref=ref, dst_ref=ref, send_sem=h_send.at[turn], recv_sem=h_recv.at[from_tp, turn],
            device_id=sibling, device_id_type=MESH,
        ).wait_recv()

    first = lax.rem(x, 2)
    own_ctx = x * 2 + core
    swap_ctx = swap_x * 2 + core

    def chunk_of(phase):
        return jnp.where(phase == 0, 0, jnp.where(phase == 1, 1, jnp.where(phase == 2, first, 1 - first)))

    def slot_of(step):
        return lax.rem(step, 4) + 4 * (step // 8)

    score(0, 0, 0)

    @pl.loop(0, 16)
    def _(step):
        phase = step // 4
        slot = slot_of(step)
        chunk = chunk_of(phase)
        later = jnp.minimum(step + 1, 15)

        @pl.when(step < 2)
        def _():
            forward(step + 2)

        @pl.when((step >= 4) & (step < 8))
        def _():
            forward(step)

        @pl.when((step < 3) | ((step >= 7) & (step < 11)))
        def _():
            prepare(slot_of(later))

        @pl.when(step == 3)
        def _():
            swap.wait_recv()
            turn_queries(1)

        score(slot, chunk * 2 + 1, 1)
        process(slot, chunk * 2, 0)
        score(slot_of(later), chunk_of(later // 4) * 2, 0)
        process(slot, chunk * 2 + 1, 1)

        @pl.when(step == 11)
        def _():
            for block in range(SPAN // BLK):
                at = pl.ds(block * BLK, BLK)
                vs_t[:HD, at] = vs_raw[at].astype(jnp.float32).T.astype(jnp.bfloat16)

        @pl.when((step == 11) | (step == 15))
        def _():
            @pl.loop(0, 2)
            def _(half):
                span_step(chunk * 2 + half, jnp.where(chunk == 0, own_ctx, swap_ctx))
                finish(chunk, half, phase - 2)

        @pl.when(step >= 14)
        def _():
            pass_on(0, step - 14)

    locals_[5].wait()
    locals_[6].wait()
    near = jnp.where(first == 0, x + 1, x - 1)

    @pl.loop(0, 2)
    def _(turn):
        mine, other = rows_of(x, turn), rows_of(near, turn)

        @pl.when(turn == 1)
        def _():
            for half in range(2):
                pass_on(turn, half)

        for half in range(2):
            arrived(4, turn, half)
        project(mine, group, False)
        for half in range(2):
            arrived(5, turn, half)
            arrived(6, turn, half)
        project(mine, 1 - group, True)
        hand_on(mine).start()
        for half in range(2):
            pass_far(turn, half)
        project(other, group, False)
        for half in range(2):
            arrived(7, turn, half)
        project(other, 1 - group, True)
        hand_on(other).start()

    @pl.loop(0, 2)
    def _(turn):
        for from_tp in range(2):
            handed(from_tp, turn)
        at = pl.ds(pl.multiple_of(turn * 256, 256), 256)
        out_ref[at] = (got[0, turn].astype(jnp.float32) + got[1, turn].astype(jnp.float32)).astype(jnp.bfloat16)

    @pl.loop(0, 2)
    def _(turn):
        for half in range(2):
            for kind in range(8):
                moved(kind, turn, half)[0].wait_send()

    @pl.loop(0, 4)
    def _(rows):
        hand_on(rows).wait_send()

    for copy in sends:
        copy.wait_send()
    swap.wait_send()

    @pl.loop(0, 8)
    def _(slot):
        forward_copy(slot).wait_send()


def layer(
    queries, span_keys, span_values, prefix_keys, prefix_values, out_weight, residual, block_slot, span_index
):
    any_spec = pl.BlockSpec(memory_space=pl.ANY)
    smem = pl.BlockSpec(memory_space=pltpu.SMEM)
    vmem = pl.BlockSpec(memory_space=pltpu.VMEM)
    dma = pltpu.SemaphoreType.DMA
    bf16, f32 = jnp.bfloat16, jnp.float32
    return pl.pallas_call(
        layer_kernel,
        out_shape=jax.ShapeDtypeStruct((512, 1024), bf16),
        in_specs=[any_spec] * 7 + [smem, smem],
        out_specs=vmem,
        scratch_shapes=[
            pltpu.VMEM((4, 2, 2, 2, BLK, 1024), bf16),
            pltpu.VMEM((4096, 1024), bf16),
            pltpu.VMEM((512, 1024), bf16),
            pltpu.VMEM((256, 1024), f32),
            pltpu.VMEM((4, 256, 1024), bf16),
            pltpu.VMEM((2, 2, 256, 1024), bf16),
            pltpu.VMEM((8, 2, 2, PRE + SPN, HD), bf16),
            pltpu.VMEM((2, BLK, 2048), bf16),
            pltpu.VMEM((2 * HD, 4 * QB), bf16),
            pltpu.VMEM((8, SLOT, 2 * HD), bf16),
            pltpu.VMEM((8, VR, SLOT), bf16),
            pltpu.VMEM((SPAN, 2 * HD), bf16),
            pltpu.VMEM((SPAN, HD), bf16),
            pltpu.VMEM((VR, SPAN), bf16),
            pltpu.VMEM((2, SLOT, QB), f32),
            pltpu.VMEM((SPAN, QB), f32),
            pltpu.VMEM((BLK, QB), f32),
            pltpu.VMEM((2, 1, QB), f32),
            pltpu.VMEM((4, 1, QB), f32),
            pltpu.VMEM((4, VR, QB), f32),
            dma((8, 4)), dma((8,)), dma((8,)), dma((8,)), dma(()), dma(()), dma((7,)),
            dma((4, 8)), dma((4, 8)), dma((4,)), dma((2, 2)),
        ],
        compiler_params=pltpu.CompilerParams(
            collective_id=0, has_side_effects=True, vmem_limit_bytes=60 << 20
        ),
        name="layer",
    )(
        queries, span_keys, span_values, prefix_keys, prefix_values, out_weight, residual, block_slot, span_index
    )


def per_device(
    queries, span_keys, span_values, prefix_keys, prefix_values, out_weight, residual, block_slot, span_index
):
    return layer(
        queries[0], span_keys[0], span_values[0], prefix_keys[0], prefix_values[0], out_weight[0], residual[0],
        block_slot, span_index,
    )[None]


def solution(mesh):
    in_specs = (
        P("section", "ctx", "tp"),
        P("section", ("ctx", "tp"), None),
        P("section", ("ctx", "tp"), None),
        P("section", ("ctx", "tp"), None),
        P("section", ("ctx", "tp"), None),
        P("section", "tp", "ctx"),
        P("section", "tp", "ctx"),
        P(),
        P("section"),
    )
    return jax.shard_map(
        per_device, mesh=mesh, in_specs=in_specs, out_specs=P("section", "tp", "ctx"), check_vma=False
    )
```

```python
import functools
import math

import jax
import jax.numpy as jnp
from jax import lax
from jax.experimental import pallas as pl
from jax.experimental.pallas import tpu as pltpu
from jax.sharding import PartitionSpec as P

MESH = pl.DeviceIdType.MESH
HD = 128
BLK = 128
HALF = 64
QB = 1024
PRE = 384
SPN = 64
ROWS = PRE + SPN
SLOT = 2 * ROWS
VR = 144
LOW = -1e30
SLOTS = ((0, 0), (0, 1), (1, 0), (2, 0), (1, 1), (2, 1), (3, 0), (3, 1))


def pick(index, table):
    value = jnp.int32(table[-1])
    for position in range(len(table) - 1):
        value = jnp.where(index == position, jnp.int32(table[position]), value)
    return value


def aligned(start, size):
    return pl.ds(pl.multiple_of(start, size), size)


def layer_kernel(
    q_hbm, sk_hbm, sv_hbm, pk_hbm, pv_hbm, w_hbm, res_hbm, slot_ref, limit_ref, out_ref,
    heads, weight, rest, total, part, got, summed, final, stage, kv, q_raw, q_t, k_two, v_t, scores, tri,
    block_max, row_max, acc,
    stage_sem, local_sem, send_sem, recv_sem, fwd_send, fwd_recv, relay_send, q_send, q_recv,
    g_send, g_recv, h_send, h_recv, z_send, z_recv,
):
    section, ctx, tp = lax.axis_index("section"), lax.axis_index("ctx"), lax.axis_index("tp")
    x, core = ctx // 2, lax.rem(ctx, 2)
    near = x + 1 - 2 * lax.rem(x, 2)
    chips = (x, near, 3 - x, 3 - near)
    group = x // 2
    odd = lax.rem(section, 2)

    def device(kind, dt=0):
        return (section, chips[kind] * 2 + core, lax.rem(tp + dt, 2))

    sibling = (section, x * 2 + 1 - core, tp)
    twin_section = section + 1 - 2 * odd
    above, below = lax.rem(section + 2, 8), lax.rem(section + 6, 8)

    barrier = pltpu.get_barrier_semaphore()
    greeted = [device(kind, dt) for kind, dt in SLOTS[1:6]] + [sibling]
    greeted += [(twin_section, ctx, half) for half in range(2)] + [(below, ctx, tp)]
    for other in greeted:
        pl.semaphore_signal(barrier, inc=1, device_id=other, device_id_type=MESH)

    def load_rows(head, dst, sem):
        cols = aligned(head * HD, HD)
        for src, which, at, rows in (
            (pk_hbm, 0, 0, PRE), (pv_hbm, 1, 0, PRE), (sk_hbm, 0, PRE, SPN), (sv_hbm, 1, PRE, SPN)
        ):
            pltpu.make_async_copy(src.at[:, cols], dst.at[which, pl.ds(at, rows)], sem).start()

    blocks = [kv.at[0, core]] + [stage.at[number] for number in range(3)]
    held = ((tp, group), (tp, 1 - group), (1 - tp, group), (1 - tp, 1 - group))
    for number, (side, which) in enumerate(held):
        load_rows(side * 2 + which, blocks[number], stage_sem.at[number])
    own_queries = pltpu.make_async_copy(q_hbm.at[:, aligned(group * 2048, 2048)], q_raw.at[0], local_sem.at[0])
    own_queries.start()

    def wait_block(number):
        pltpu.make_async_copy(blocks[number], blocks[number], stage_sem.at[number]).wait()

    swap = pltpu.make_async_remote_copy(
        src_ref=q_hbm.at[:, aligned((1 - group) * 2048, 2048)], dst_ref=q_raw.at[1], send_sem=q_send,
        recv_sem=q_recv, device_id=device(2), device_id_type=MESH,
    )

    def row_send(slot):
        kind, dt = SLOTS[slot]
        return pltpu.make_async_remote_copy(
            src_ref=blocks[2 * dt + (kind == 2)], dst_ref=kv.at[slot, core], send_sem=send_sem.at[slot],
            recv_sem=recv_sem.at[slot], device_id=device(kind, dt), device_id_type=MESH,
        )

    def relay(slot, to):
        return pltpu.make_async_remote_copy(
            src_ref=kv.at[slot, core], dst_ref=kv.at[to, core], send_sem=relay_send.at[to - 6],
            recv_sem=recv_sem.at[to], device_id=device(1), device_id_type=MESH,
        )

    def to_sibling(slot):
        return pltpu.make_async_remote_copy(
            src_ref=kv.at[slot, core], dst_ref=kv.at[slot, core], send_sem=fwd_send.at[slot],
            recv_sem=fwd_recv.at[slot], device_id=sibling, device_id_type=MESH,
        )

    def arrived_sibling(slot):
        ref = kv.at[slot, 1 - core]
        pltpu.make_async_remote_copy(
            src_ref=ref, dst_ref=ref, send_sem=fwd_send.at[slot], recv_sem=fwd_recv.at[slot],
            device_id=sibling, device_id_type=MESH,
        ).wait_recv()

    def forward(slot):
        pltpu.make_async_copy(kv.at[slot, core], kv.at[slot, core], recv_sem.at[slot]).wait()
        to_sibling(slot).start()

    for number in range(4):
        wait_block(number)
    pl.semaphore_wait(barrier, len(greeted))
    for slot in (3, 2, 1):
        row_send(slot).start()
    to_sibling(0).start()
    load_weight = pltpu.make_async_copy(w_hbm, weight, local_sem.at[1])
    load_rest = pltpu.make_async_copy(res_hbm, rest, local_sem.at[2])
    load_weight.start()
    load_rest.start()

    def source(slot):
        kind = pick(slot, [s[0] for s in SLOTS])
        dt = pick(slot, [s[1] for s in SLOTS])
        chip = jnp.where(kind == 0, x, jnp.where(kind == 1, near, jnp.where(kind == 2, 3 - x, 3 - near)))
        return chip, lax.rem(tp + dt, 2)

    def prepare(slot):
        for c in range(2):
            for start, size, at in ((0, PRE, c * PRE), (PRE, SPN, 2 * PRE + c * SPN)):
                keys = kv[slot, c, 0, pl.ds(start, size)]
                k_two[slot, pl.ds(at, size), :HD] = keys
                k_two[slot, pl.ds(at, size), HD:] = keys
            for page in range(PRE // BLK):
                v_t[slot, :HD, pl.ds(c * PRE + page * BLK, BLK)] = kv[slot, c, 1, pl.ds(page * BLK, BLK)].T
        span_values = jnp.concatenate([kv[slot, c, 1, pl.ds(PRE, SPN)] for c in range(2)], axis=0)
        v_t[slot, :HD, pl.ds(2 * PRE, BLK)] = span_values.T

    def turn_queries(chunk):
        scale = math.log2(math.e) / math.sqrt(HD)

        @pl.loop(0, 8)
        def _(pair):
            for half in range(2):
                rows = pl.ds(half * HALF, HALF)
                block = jnp.concatenate(
                    [q_raw[chunk, rows, aligned((2 * pair + one) * HD, HD)] for one in range(2)], axis=0
                )
                turned = (block.astype(jnp.float32) * scale).T
                high = turned.astype(jnp.bfloat16)
                at = aligned((chunk * 2 + half) * QB + pair * HD, HD)
                q_t[:HD, at] = high
                q_t[HD:, at] = (turned - high.astype(jnp.float32)).astype(jnp.bfloat16)

    ones = jnp.ones((VR - HD, SLOT), jnp.bfloat16)
    for slot in range(8):
        v_t[slot, HD:] = ones
    key_at = lax.broadcasted_iota(jnp.int32, (SPN, QB), 0)
    row_at = lax.rem(lax.broadcasted_iota(jnp.int32, (SPN, QB), 1), HALF)
    tri[0] = jnp.zeros((SPN, QB), jnp.float32)
    tri[1] = jnp.where(key_at <= row_at, 0.0, LOW)
    row_max[...] = jnp.full(row_max.shape, LOW, jnp.float32)

    @pl.loop(0, 4)
    def _(q):
        acc[q] = jnp.zeros((VR, QB), jnp.float32)

    own_queries.wait()
    turn_queries(0)
    arrived_sibling(0)
    prepare(0)

    limit = limit_ref[0] * 8

    def masks(slot, q):
        chip, side = source(slot)
        row_block = jnp.where(q < 2, x, 3 - x) * 4 + core * 2 + lax.rem(q, 2)
        found = []
        for c in range(2):
            for page in range(PRE // BLK):
                number = ((chip * 2 + c) * 2 + side) * (PRE // BLK) + page
                found.append((c * PRE + page * BLK, BLK, slot_ref[number] < limit, None))
        for c in range(2):
            key_block = (chip * 2 + c) * 2 + side
            diagonal = jnp.where(key_block == row_block, 1, 0)
            found.append((2 * PRE + c * SPN, SPN, key_block <= row_block, diagonal))
        return found

    def score(slot, q, buffer):
        value = jnp.dot(k_two[slot], q_t[:, aligned(q * QB, QB)], preferred_element_type=jnp.float32)
        largest = jnp.full((1, QB), LOW, jnp.float32)
        for start, rows, visible, diagonal in masks(slot, q):
            block = value[start : start + rows]
            if diagonal is not None:
                block = block + tri[diagonal]
            scores[buffer, start : start + rows] = block
            largest = jnp.maximum(largest, jnp.where(visible, jnp.max(block, axis=0, keepdims=True), LOW))
        block_max[buffer] = largest

    def process(slot, q, buffer):
        before = row_max[q]
        now = jnp.maximum(before, block_max[buffer])
        row_max[q] = now
        weights = jnp.concatenate(
            [
                jnp.exp2(scores[buffer, start : start + rows] - jnp.where(visible, now, -LOW)).astype(jnp.bfloat16)
                for start, rows, visible, _ in masks(slot, q)
            ],
            axis=0,
        )
        added = jnp.dot(v_t[slot], weights, preferred_element_type=jnp.float32)
        acc[q] = acc[q] * jnp.exp2(before - now) + added

    def place(chip, turn, half, c):
        return heads.at[jnp.where(turn == 0, chip, 3 - chip), chip // 2, half, c]

    def moved(kind, turn, half):
        if kind < 2:
            to = device(kind + 1)
            src, dst = place(x, turn, half, core), place(chips[kind + 1], turn, half, core)
        elif kind < 4:
            to = device(kind - 1)
            rows = pl.ds((kind - 2) * (HALF // 2), HALF // 2)
            src, dst = (place(chip, turn, half, core).at[rows] for chip in (chips[4 - kind], chips[3]))
        else:
            to = sibling
            src, dst = (place(chips[kind - 4], turn, half, c) for c in (core, 1 - core))
        piece = turn * 2 + half
        make = functools.partial(
            pltpu.make_async_remote_copy, send_sem=g_send.at[piece, kind], recv_sem=g_recv.at[piece, kind],
            device_id=to, device_id_type=MESH,
        )
        return make(src_ref=src, dst_ref=src), make(src_ref=dst, dst_ref=dst)

    def send(kind, turn, half):
        moved(kind, turn, half)[0].start()

    def arrived(kind, turn, half):
        moved(kind, turn, half)[1].wait_recv()

    def finish(turn, half):
        q = turn * 2 + half
        share = 1.0 / acc[q, HD : HD + 1]
        mine = place(x, turn, half, core)
        for pair in range(8):
            at = slice(pair * HD, (pair + 1) * HD)
            block = (acc[q, :HD, at] * share[:, at]).T.astype(jnp.bfloat16)
            for one in range(2):
                mine[:, pl.ds((2 * pair + one) * HD, HD)] = block[one * HALF : (one + 1) * HALF]
        for kind in (0, 1, 4):
            send(kind, turn, half)

    def pass_on(turn, half):
        arrived(1, turn, half)
        send(2, turn, half)
        send(6, turn, half)
        arrived(0, turn, half)
        send(3, turn, half)
        send(5, turn, half)

    def pass_far(turn, half):
        arrived(2, turn, half)
        arrived(3, turn, half)
        send(7, turn, half)

    def first_part(kind):
        chip = chips[kind]
        for half in range(2):
            arrived(kind + 4, 0, half)
        depth = aligned((chip // 2) * 2048, 2048)

        @pl.loop(0, 4)
        def _(number):
            cols = aligned(number * 256, 256)
            total[chip, :, cols] = jnp.dot(
                heads[chip, chip // 2].reshape(256, 2048), weight[depth, cols], preferred_element_type=jnp.float32
            )

    def hand_on(rows, half):
        return pltpu.make_async_remote_copy(
            src_ref=part.at[rows, half], dst_ref=got.at[tp, lax.rem(rows, 2), half], send_sem=h_send.at[rows, half],
            recv_sem=h_recv.at[tp, lax.rem(rows, 2), half], device_id=(twin_section, ctx, rows // 2),
            device_id_type=MESH,
        )

    def second_part(kind, half):
        chip = chips[kind]
        rows = 3 - chip
        arrived(kind + 4, 1, half)
        depth = aligned((chip // 2) * 2048, 2048)

        @pl.loop(0, 4)
        def _(number):
            cols = aligned(number * 256, 256)
            value = jnp.dot(
                heads[rows, chip // 2, half].reshape(BLK, 2048), weight[depth, cols],
                preferred_element_type=jnp.float32,
            )
            extra = jnp.concatenate(
                [
                    rest[aligned(lax.rem(rows, 2) * 256 + c * BLK + half * HALF, HALF), cols].astype(jnp.float32)
                    for c in range(2)
                ],
                axis=0,
            )
            value = value + total[rows, pl.ds(half * BLK, BLK), cols] + jnp.where(rows // 2 == tp, extra, 0.0)
            part[rows, half, :, cols] = value.astype(jnp.bfloat16)

        hand_on(rows, half).start()

    def climb(which, half):
        return pltpu.make_async_remote_copy(
            src_ref=summed.at[which, half], dst_ref=final.at[which, half], send_sem=z_send.at[which, half],
            recv_sem=z_recv.at[which, half], device_id=(above, ctx, tp), device_id_type=MESH,
        )

    def collect(which, half):
        for side in range(2):
            ref = got.at[side, which, half]
            pltpu.make_async_remote_copy(
                src_ref=ref, dst_ref=ref, send_sem=h_send.at[which, half], recv_sem=h_recv.at[side, which, half],
                device_id=sibling, device_id_type=MESH,
            ).wait_recv()
        both = got[0, which, half].astype(jnp.float32) + got[1, which, half].astype(jnp.float32)
        summed[which, half] = both.astype(jnp.bfloat16)

        @pl.when(odd == 0)
        def _():
            climb(which, half).start()

    def step_at(number):
        slot = jnp.where(number < 16, number // 2, lax.rem(number, 8))
        return slot, jnp.where(number < 16, lax.rem(number, 2), number // 8)

    score(0, 0, 0)

    @pl.loop(0, 8)
    def _(slot):
        for at, slots in ((0, (1,)), (1, (3, 2)), (3, (5, 4)), (5, (6,)), (6, (7,))):

            @pl.when(slot == at)
            def _():
                for which in slots:
                    forward(which)
                if at == 1:
                    relay(3, 6).start()
                    row_send(5).start()
                    row_send(4).start()
                    swap.start()
                if at == 3:
                    relay(5, 7).start()

        @pl.when(slot < 7)
        def _():
            arrived_sibling(slot + 1)

        prepare(jnp.minimum(slot + 1, 7))
        score(slot, 1, 1)
        process(slot, 0, 0)

        @pl.when(slot == 7)
        def _():
            swap.wait_recv()
            turn_queries(1)

        score(*step_at(2 * slot + 2), 0)
        process(slot, 1, 1)

    for half in range(2):
        finish(0, half)

    @pl.loop(8, 16)
    def _(turn):
        @pl.when(turn == 11)
        def _():
            pass_on(0, 0)

        @pl.when(turn == 13)
        def _():
            pass_on(0, 1)

        @pl.when(turn == 14)
        def _():
            first_part(2)
            second_part(0, 0)

        score(*step_at(2 * turn + 1), 1)
        process(*step_at(2 * turn), 0)
        score(*step_at(jnp.minimum(2 * turn + 2, 31)), 0)
        process(*step_at(2 * turn + 1), 1)

        @pl.when(turn == 11)
        def _():
            finish(1, 0)

        @pl.when(turn == 10)
        def _():
            load_weight.wait()
            load_rest.wait()

    finish(1, 1)
    for half in range(2):
        pass_far(0, half)
    first_part(0)
    pass_on(1, 0)
    second_part(0, 1)
    second_part(2, 0)
    first_part(3)
    second_part(1, 0)
    first_part(1)
    pass_on(1, 1)
    pass_far(1, 0)
    second_part(3, 0)
    second_part(2, 1)
    second_part(1, 1)
    early = jnp.where(tp == (3 - x) // 2, lax.rem(3 - x, 2), lax.rem(x, 2))
    collect(early, 0)
    pass_far(1, 1)
    second_part(3, 1)
    collect(1 - early, 0)
    collect(early, 1)
    collect(1 - early, 1)

    def write(ref, which, half):
        for c in range(2):
            out_ref[aligned(which * 256 + c * BLK + half * HALF, HALF)] = ref[which, half, pl.ds(c * HALF, HALF)]

    @pl.loop(0, 4)
    def _(number):
        which, half = number // 2, lax.rem(number, 2)

        @pl.when(odd == 0)
        def _():
            climb(which, half).wait_recv()
            write(final, which, half)

        @pl.when(odd == 1)
        def _():
            write(summed, which, half)

    for slot in range(1, 6):
        row_send(slot).wait_send()
    relay(3, 6).wait_send()
    relay(5, 7).wait_send()
    swap.wait_send()

    @pl.loop(0, 8)
    def _(slot):
        to_sibling(slot).wait_send()

    @pl.loop(0, 4)
    def _(piece):
        for kind in range(8):
            moved(kind, piece // 2, lax.rem(piece, 2))[0].wait_send()

        for half in range(2):
            hand_on(piece, half).wait_send()

        @pl.when(odd == 0)
        def _():
            climb(piece // 2, lax.rem(piece, 2)).wait_send()


def layer(
    queries, span_keys, span_values, prefix_keys, prefix_values, out_weight, residual, block_slot, span_index
):
    any_spec = pl.BlockSpec(memory_space=pl.ANY)
    smem = pl.BlockSpec(memory_space=pltpu.SMEM)
    vmem = pl.BlockSpec(memory_space=pltpu.VMEM)
    dma = pltpu.SemaphoreType.DMA
    bf16, f32 = jnp.bfloat16, jnp.float32
    return pl.pallas_call(
        layer_kernel,
        out_shape=jax.ShapeDtypeStruct((512, 1024), bf16),
        in_specs=[any_spec] * 7 + [smem, smem],
        out_specs=vmem,
        scratch_shapes=[
            pltpu.VMEM((4, 2, 2, 2, HALF, 2048), bf16),
            pltpu.VMEM((4096, 1024), bf16),
            pltpu.VMEM((512, 1024), bf16),
            pltpu.VMEM((4, 256, 1024), f32),
            pltpu.VMEM((4, 2, BLK, 1024), bf16),
            pltpu.VMEM((2, 2, 2, BLK, 1024), bf16),
            pltpu.VMEM((2, 2, BLK, 1024), bf16),
            pltpu.VMEM((2, 2, BLK, 1024), bf16),
            pltpu.VMEM((3, 2, ROWS, HD), bf16),
            pltpu.VMEM((8, 2, 2, ROWS, HD), bf16),
            pltpu.VMEM((2, BLK, 2048), bf16),
            pltpu.VMEM((2 * HD, 4 * QB), bf16),
            pltpu.VMEM((8, SLOT, 2 * HD), bf16),
            pltpu.VMEM((8, VR, SLOT), bf16),
            pltpu.VMEM((2, SLOT, QB), f32),
            pltpu.VMEM((2, SPN, QB), f32),
            pltpu.VMEM((2, 1, QB), f32),
            pltpu.VMEM((4, 1, QB), f32),
            pltpu.VMEM((4, VR, QB), f32),
            dma((4,)), dma((3,)), dma((6,)), dma((8,)), dma((8,)), dma((8,)), dma((2,)), dma(()), dma(()),
            dma((4, 8)), dma((4, 8)), dma((4, 2)), dma((2, 2, 2)), dma((2, 2)), dma((2, 2)),
        ],
        compiler_params=pltpu.CompilerParams(
            collective_id=0, has_side_effects=True, vmem_limit_bytes=60 << 20
        ),
        name="layer",
    )(
        queries, span_keys, span_values, prefix_keys, prefix_values, out_weight, residual, block_slot, span_index
    )


def per_device(
    queries, span_keys, span_values, prefix_keys, prefix_values, out_weight, residual, block_slot, span_index
):
    return layer(
        queries[0], span_keys[0], span_values[0], prefix_keys[0], prefix_values[0], out_weight[0], residual[0],
        block_slot, span_index,
    )[None]


def solution(mesh):
    in_specs = (
        P("section", "ctx", "tp"),
        P("section", ("ctx", "tp"), None),
        P("section", ("ctx", "tp"), None),
        P("section", ("ctx", "tp"), None),
        P("section", ("ctx", "tp"), None),
        P("section", "tp", "ctx"),
        P("section", "tp", "ctx"),
        P(),
        P("section"),
    )
    return jax.shard_map(
        per_device, mesh=mesh, in_specs=in_specs, out_specs=P("section", "tp", "ctx"), check_vma=False
    )
```

```python
import functools
import math

import jax
import jax.numpy as jnp
from jax import lax
from jax.experimental import pallas as pl
from jax.experimental.pallas import tpu as pltpu
from jax.sharding import PartitionSpec as P

MESH = pl.DeviceIdType.MESH
HD = 128
BLK = 128
HALF = 64
QB = 1024
PRE = 384
SPN = 64
ROWS = PRE + SPN
SLOT = 2 * ROWS
VR = 144
LOW = -1e30
SLOTS = ((0, 0), (1, 0), (2, 0), (0, 1), (1, 1), (3, 0), (2, 1), (3, 1))
SENT = (1, 2, 3, 4, 6)


def pick(index, table):
    value = jnp.int32(table[-1])
    for position in range(len(table) - 1):
        value = jnp.where(index == position, jnp.int32(table[position]), value)
    return value


def aligned(start, size):
    return pl.ds(pl.multiple_of(start, size), size)


def layer_kernel(
    q_hbm, sk_hbm, sv_hbm, pk_hbm, pv_hbm, w_hbm, res_hbm, slot_ref, limit_ref, out_ref,
    heads, weight, rest, total, part, got, summed, final, stage, kv, q_raw, q_t, k_two, v_t, scores, tri,
    block_max, row_max, acc,
    stage_sem, local_sem, send_sem, recv_sem, fwd_send, fwd_recv, relay_send, q_send, q_recv,
    g_send, g_recv, h_send, h_recv, z_send, z_recv,
):
    section, ctx, tp = lax.axis_index("section"), lax.axis_index("ctx"), lax.axis_index("tp")
    x, core = ctx // 2, lax.rem(ctx, 2)
    near = x + 1 - 2 * lax.rem(x, 2)
    chips = (x, near, 3 - x, 3 - near)
    group = x // 2
    odd = lax.rem(section, 2)

    def device(kind, dt=0):
        return (section, chips[kind] * 2 + core, lax.rem(tp + dt, 2))

    sibling = (section, x * 2 + 1 - core, tp)
    twin_section = section + 1 - 2 * odd
    above, below = lax.rem(section + 2, 8), lax.rem(section + 6, 8)

    barrier = pltpu.get_barrier_semaphore()
    greeted = [device(*SLOTS[slot]) for slot in SENT] + [sibling]
    greeted += [(twin_section, ctx, half) for half in range(2)] + [(below, ctx, tp)]
    for other in greeted:
        pl.semaphore_signal(barrier, inc=1, device_id=other, device_id_type=MESH)

    def load_rows(head, dst, sem):
        cols = aligned(head * HD, HD)
        for src, which, at, rows in (
            (pk_hbm, 0, 0, PRE), (pv_hbm, 1, 0, PRE), (sk_hbm, 0, PRE, SPN), (sv_hbm, 1, PRE, SPN)
        ):
            pltpu.make_async_copy(src.at[:, cols], dst.at[which, pl.ds(at, rows)], sem).start()

    blocks = [kv.at[0, core]] + [stage.at[number] for number in range(3)]
    held = ((tp, group), (tp, 1 - group), (1 - tp, group), (1 - tp, 1 - group))
    for number, (side, which) in enumerate(held):
        load_rows(side * 2 + which, blocks[number], stage_sem.at[number])
    own_queries = pltpu.make_async_copy(q_hbm.at[:, aligned(group * 2048, 2048)], q_raw.at[0], local_sem.at[0])
    own_queries.start()

    def wait_block(number):
        pltpu.make_async_copy(blocks[number], blocks[number], stage_sem.at[number]).wait()

    swap = pltpu.make_async_remote_copy(
        src_ref=q_hbm.at[:, aligned((1 - group) * 2048, 2048)], dst_ref=q_raw.at[1], send_sem=q_send,
        recv_sem=q_recv, device_id=device(2), device_id_type=MESH,
    )

    def row_send(slot):
        kind, dt = SLOTS[slot]
        return pltpu.make_async_remote_copy(
            src_ref=blocks[2 * dt + (kind == 2)], dst_ref=kv.at[slot, core], send_sem=send_sem.at[slot],
            recv_sem=recv_sem.at[slot], device_id=device(kind, dt), device_id_type=MESH,
        )

    def relay(slot, to):
        return pltpu.make_async_remote_copy(
            src_ref=kv.at[slot, core], dst_ref=kv.at[to, core], send_sem=relay_send.at[to // 7],
            recv_sem=recv_sem.at[to], device_id=device(1), device_id_type=MESH,
        )

    def to_sibling(slot):
        return pltpu.make_async_remote_copy(
            src_ref=kv.at[slot, core], dst_ref=kv.at[slot, core], send_sem=fwd_send.at[slot],
            recv_sem=fwd_recv.at[slot], device_id=sibling, device_id_type=MESH,
        )

    def arrived_sibling(slot):
        ref = kv.at[slot, 1 - core]
        pltpu.make_async_remote_copy(
            src_ref=ref, dst_ref=ref, send_sem=fwd_send.at[slot], recv_sem=fwd_recv.at[slot],
            device_id=sibling, device_id_type=MESH,
        ).wait_recv()

    def forward(slot):
        pltpu.make_async_copy(kv.at[slot, core], kv.at[slot, core], recv_sem.at[slot]).wait()
        to_sibling(slot).start()

    for number in range(4):
        wait_block(number)
    pl.semaphore_wait(barrier, len(greeted))
    for slot in (2, 1, 3):
        row_send(slot).start()
    to_sibling(0).start()
    load_weight = pltpu.make_async_copy(w_hbm, weight, local_sem.at[1])
    load_rest = pltpu.make_async_copy(res_hbm, rest, local_sem.at[2])
    load_weight.start()
    load_rest.start()

    def source(slot):
        kind = pick(slot, [s[0] for s in SLOTS])
        dt = pick(slot, [s[1] for s in SLOTS])
        chip = jnp.where(kind == 0, x, jnp.where(kind == 1, near, jnp.where(kind == 2, 3 - x, 3 - near)))
        return chip, lax.rem(tp + dt, 2)

    def prepare(slot):
        for c in range(2):
            for start, size, at in ((0, PRE, c * PRE), (PRE, SPN, 2 * PRE + c * SPN)):
                keys = kv[slot, c, 0, pl.ds(start, size)]
                k_two[slot, pl.ds(at, size), :HD] = keys
                k_two[slot, pl.ds(at, size), HD:] = keys
            for page in range(PRE // BLK):
                v_t[slot, :HD, pl.ds(c * PRE + page * BLK, BLK)] = kv[slot, c, 1, pl.ds(page * BLK, BLK)].T
        span_values = jnp.concatenate([kv[slot, c, 1, pl.ds(PRE, SPN)] for c in range(2)], axis=0)
        v_t[slot, :HD, pl.ds(2 * PRE, BLK)] = span_values.T

    def turn_queries(chunk):
        scale = math.log2(math.e) / math.sqrt(HD)

        @pl.loop(0, 8)
        def _(pair):
            for half in range(2):
                rows = pl.ds(half * HALF, HALF)
                block = jnp.concatenate(
                    [q_raw[chunk, rows, aligned((2 * pair + one) * HD, HD)] for one in range(2)], axis=0
                )
                turned = (block.astype(jnp.float32) * scale).T
                high = turned.astype(jnp.bfloat16)
                at = aligned((chunk * 2 + half) * QB + pair * HD, HD)
                q_t[:HD, at] = high
                q_t[HD:, at] = (turned - high.astype(jnp.float32)).astype(jnp.bfloat16)

    ones = jnp.ones((VR - HD, SLOT), jnp.bfloat16)
    for slot in range(8):
        v_t[slot, HD:] = ones
    key_at = lax.broadcasted_iota(jnp.int32, (SPN, QB), 0)
    row_at = lax.rem(lax.broadcasted_iota(jnp.int32, (SPN, QB), 1), HALF)
    tri[0] = jnp.zeros((SPN, QB), jnp.float32)
    tri[1] = jnp.where(key_at <= row_at, 0.0, LOW)
    row_max[...] = jnp.full(row_max.shape, LOW, jnp.float32)

    @pl.loop(0, 4)
    def _(q):
        acc[q] = jnp.zeros((VR, QB), jnp.float32)

    own_queries.wait()
    turn_queries(0)
    arrived_sibling(0)
    prepare(0)

    limit = limit_ref[0] * 8

    def masks(slot, q):
        chip, side = source(slot)
        row_block = jnp.where(q < 2, x, 3 - x) * 4 + core * 2 + lax.rem(q, 2)
        found = []
        for c in range(2):
            for page in range(PRE // BLK):
                number = ((chip * 2 + c) * 2 + side) * (PRE // BLK) + page
                found.append((c * PRE + page * BLK, BLK, slot_ref[number] < limit, None))
        for c in range(2):
            key_block = (chip * 2 + c) * 2 + side
            diagonal = jnp.where(key_block == row_block, 1, 0)
            found.append((2 * PRE + c * SPN, SPN, key_block <= row_block, diagonal))
        return found

    def score(slot, q, buffer):
        value = jnp.dot(k_two[slot], q_t[:, aligned(q * QB, QB)], preferred_element_type=jnp.float32)
        largest = jnp.full((1, QB), LOW, jnp.float32)
        for start, rows, visible, diagonal in masks(slot, q):
            block = value[start : start + rows]
            if diagonal is not None:
                block = block + tri[diagonal]
            scores[buffer, start : start + rows] = block
            largest = jnp.maximum(largest, jnp.where(visible, jnp.max(block, axis=0, keepdims=True), LOW))
        block_max[buffer] = largest

    def process(slot, q, buffer):
        before = row_max[q]
        now = jnp.maximum(before, block_max[buffer])
        row_max[q] = now
        weights = jnp.concatenate(
            [
                jnp.exp2(scores[buffer, start : start + rows] - jnp.where(visible, now, -LOW)).astype(jnp.bfloat16)
                for start, rows, visible, _ in masks(slot, q)
            ],
            axis=0,
        )
        added = jnp.dot(v_t[slot], weights, preferred_element_type=jnp.float32)
        acc[q] = acc[q] * jnp.exp2(before - now) + added

    def place(chip, turn, half, c):
        return heads.at[jnp.where(turn == 0, chip, 3 - chip), chip // 2, half, c]

    def moved(kind, turn, half):
        if kind < 2:
            to = device(kind + 1)
            src, dst = place(x, turn, half, core), place(chips[kind + 1], turn, half, core)
        elif kind < 4:
            to = device(kind - 1)
            rows = pl.ds((kind - 2) * (HALF // 2), HALF // 2)
            src, dst = (place(chip, turn, half, core).at[rows] for chip in (chips[4 - kind], chips[3]))
        else:
            to = sibling
            src, dst = (place(chips[kind - 4], turn, half, c) for c in (core, 1 - core))
        piece = turn * 2 + half
        make = functools.partial(
            pltpu.make_async_remote_copy, send_sem=g_send.at[piece, kind], recv_sem=g_recv.at[piece, kind],
            device_id=to, device_id_type=MESH,
        )
        return make(src_ref=src, dst_ref=src), make(src_ref=dst, dst_ref=dst)

    def send(kind, turn, half):
        moved(kind, turn, half)[0].start()

    def arrived(kind, turn, half):
        moved(kind, turn, half)[1].wait_recv()

    def finish(turn, half):
        q = turn * 2 + half
        share = 1.0 / acc[q, HD : HD + 1]
        mine = place(x, turn, half, core)
        for pair in range(8):
            at = slice(pair * HD, (pair + 1) * HD)
            block = (acc[q, :HD, at] * share[:, at]).T.astype(jnp.bfloat16)
            for one in range(2):
                mine[:, pl.ds((2 * pair + one) * HD, HD)] = block[one * HALF : (one + 1) * HALF]

    def publish(turn, half):
        for kind in (0, 1, 4):
            send(kind, turn, half)

    def pass_on(turn, half):
        arrived(1, turn, half)
        send(2, turn, half)
        send(6, turn, half)
        arrived(0, turn, half)
        send(3, turn, half)
        send(5, turn, half)

    def pass_far(turn, half):
        arrived(2, turn, half)
        arrived(3, turn, half)
        send(7, turn, half)

    def first_part(kind):
        chip = chips[kind]
        for half in range(2):
            arrived(kind + 4, 0, half)
        depth = aligned((chip // 2) * 2048, 2048)

        @pl.loop(0, 2)
        def _(number):
            cols = aligned(number * 512, 512)
            total[chip, :, cols] = jnp.dot(
                heads[chip, chip // 2].reshape(256, 2048), weight[depth, cols], preferred_element_type=jnp.float32
            )

    def hand_on(rows, half, side):
        here = (tp, lax.rem(rows, 2), half, side)
        return pltpu.make_async_remote_copy(
            src_ref=part.at[rows, half, side], dst_ref=got.at[here], send_sem=h_send.at[rows, half, side],
            recv_sem=h_recv.at[here], device_id=(twin_section, ctx, rows // 2), device_id_type=MESH,
        )

    def second_part(kind, half):
        chip = chips[kind]
        rows = 3 - chip
        arrived(kind + 4, 1, half)
        depth = aligned((chip // 2) * 2048, 2048)

        @pl.loop(0, 2)
        def _(number):
            cols = aligned(number * 512, 512)
            value = jnp.dot(
                heads[rows, chip // 2, half].reshape(BLK, 2048), weight[depth, cols],
                preferred_element_type=jnp.float32,
            )
            extra = jnp.concatenate(
                [
                    rest[aligned(lax.rem(rows, 2) * 256 + c * BLK + half * HALF, HALF), cols].astype(jnp.float32)
                    for c in range(2)
                ],
                axis=0,
            )
            value = value + total[rows, pl.ds(half * BLK, BLK), cols] + jnp.where(rows // 2 == tp, extra, 0.0)
            part[rows, half, number] = value.astype(jnp.bfloat16)
            hand_on(rows, half, number).start()

    def climb(unit):
        return pltpu.make_async_remote_copy(
            src_ref=summed.at[unit], dst_ref=final.at[unit], send_sem=z_send.at[unit], recv_sem=z_recv.at[unit],
            device_id=(above, ctx, tp), device_id_type=MESH,
        )

    def collect(which, half):
        @pl.loop(0, 2)
        def _(side):
            unit = (which, half, side)
            for origin in range(2):
                place_of = (origin, *unit)
                ref = got.at[place_of]
                pltpu.make_async_remote_copy(
                    src_ref=ref, dst_ref=ref, send_sem=h_send.at[unit], recv_sem=h_recv.at[place_of],
                    device_id=sibling, device_id_type=MESH,
                ).wait_recv()
            both = got[(0, *unit)].astype(jnp.float32) + got[(1, *unit)].astype(jnp.float32)
            summed[unit] = both.astype(jnp.bfloat16)

            @pl.when(odd == 0)
            def _():
                climb(unit).start()

    def step_at(number):
        slot = jnp.where(number < 16, number // 2, lax.rem(number, 8))
        return slot, jnp.where(number < 16, lax.rem(number, 2), number // 8)

    score(0, 0, 0)

    @pl.loop(0, 8)
    def _(slot):
        for at, slots in ((2, (3,)), (3, (6, 4)), (4, (5,)), (6, (7,))):

            @pl.when(slot == at)
            def _():
                for which in slots:
                    forward(which)
                    if which == 6:
                        relay(6, 7).start()

        score(slot, 1, 1)
        process(slot, 0, 0)

        @pl.when(slot == 0)
        def _():
            forward(1)
            forward(2)
            relay(2, 5).start()
            row_send(6).start()
            row_send(4).start()
            swap.start()

        @pl.when(slot < 7)
        def _():
            arrived_sibling(slot + 1)

        @pl.when(slot == 7)
        def _():
            swap.wait_recv()
            turn_queries(1)

        prepare(jnp.minimum(slot + 1, 7))
        score(*step_at(2 * slot + 2), 0)
        process(slot, 1, 1)

    for half in range(2):
        finish(0, half)
        publish(0, half)

    @pl.loop(8, 16)
    def _(turn):
        @pl.when(turn == 12)
        def _():
            pass_on(0, 0)

        @pl.when(turn == 13)
        def _():
            pass_on(0, 1)

        @pl.when(turn == 14)
        def _():
            first_part(2)
            second_part(0, 0)

        score(*step_at(2 * turn + 1), 1)
        process(*step_at(2 * turn), 0)
        score(*step_at(jnp.minimum(2 * turn + 2, 31)), 0)
        process(*step_at(2 * turn + 1), 1)

        @pl.when(turn == 11)
        def _():
            finish(1, 0)
            publish(1, 0)

        @pl.when(turn == 10)
        def _():
            load_weight.wait()
            load_rest.wait()

    finish(1, 1)
    for half in range(2):
        pass_far(0, half)
    first_part(0)
    pass_on(1, 0)
    publish(1, 1)
    second_part(2, 0)
    first_part(3)
    second_part(1, 0)
    first_part(1)
    pass_far(1, 0)
    second_part(3, 0)
    second_part(0, 1)
    early = jnp.where(tp == (3 - x) // 2, lax.rem(3 - x, 2), lax.rem(x, 2))
    collect(early, 0)
    pass_on(1, 1)
    second_part(2, 1)
    second_part(1, 1)
    collect(1 - early, 0)
    pass_far(1, 1)
    second_part(3, 1)
    collect(early, 1)
    collect(1 - early, 1)

    def write(ref, unit):
        which, half, side = unit
        for c in range(2):
            rows = aligned(which * 256 + c * BLK + half * HALF, HALF)
            out_ref[rows, aligned(side * 512, 512)] = ref[(*unit, pl.ds(c * HALF, HALF))]

    @pl.loop(0, 8)
    def _(number):
        half, which, side = number // 4, lax.rem(number // 2, 2), lax.rem(number, 2)
        unit = (which, half, side)

        @pl.when(odd == 0)
        def _():
            climb(unit).wait_recv()
            write(final, unit)

        @pl.when(odd == 1)
        def _():
            write(summed, unit)

    for slot in SENT:
        row_send(slot).wait_send()
    relay(2, 5).wait_send()
    relay(6, 7).wait_send()
    swap.wait_send()

    @pl.loop(0, 8)
    def _(slot):
        to_sibling(slot).wait_send()

    @pl.loop(0, 4)
    def _(piece):
        for kind in range(8):
            moved(kind, piece // 2, lax.rem(piece, 2))[0].wait_send()

        for half in range(2):
            for side in range(2):
                hand_on(piece, half, side).wait_send()

        @pl.when(odd == 0)
        def _():
            for side in range(2):
                climb((piece // 2, lax.rem(piece, 2), side)).wait_send()


def layer(
    queries, span_keys, span_values, prefix_keys, prefix_values, out_weight, residual, block_slot, span_index
):
    any_spec = pl.BlockSpec(memory_space=pl.ANY)
    smem = pl.BlockSpec(memory_space=pltpu.SMEM)
    vmem = pl.BlockSpec(memory_space=pltpu.VMEM)
    dma = pltpu.SemaphoreType.DMA
    bf16, f32 = jnp.bfloat16, jnp.float32
    return pl.pallas_call(
        layer_kernel,
        out_shape=jax.ShapeDtypeStruct((512, 1024), bf16),
        in_specs=[any_spec] * 7 + [smem, smem],
        out_specs=vmem,
        scratch_shapes=[
            pltpu.VMEM((4, 2, 2, 2, HALF, 2048), bf16),
            pltpu.VMEM((4096, 1024), bf16),
            pltpu.VMEM((512, 1024), bf16),
            pltpu.VMEM((4, 256, 1024), f32),
            pltpu.VMEM((4, 2, 2, BLK, 512), bf16),
            pltpu.VMEM((2, 2, 2, 2, BLK, 512), bf16),
            pltpu.VMEM((2, 2, 2, BLK, 512), bf16),
            pltpu.VMEM((2, 2, 2, BLK, 512), bf16),
            pltpu.VMEM((3, 2, ROWS, HD), bf16),
            pltpu.VMEM((8, 2, 2, ROWS, HD), bf16),
            pltpu.VMEM((2, BLK, 2048), bf16),
            pltpu.VMEM((2 * HD, 4 * QB), bf16),
            pltpu.VMEM((8, SLOT, 2 * HD), bf16),
            pltpu.VMEM((8, VR, SLOT), bf16),
            pltpu.VMEM((2, SLOT, QB), f32),
            pltpu.VMEM((2, SPN, QB), f32),
            pltpu.VMEM((2, 1, QB), f32),
            pltpu.VMEM((4, 1, QB), f32),
            pltpu.VMEM((4, VR, QB), f32),
            dma((4,)), dma((3,)), dma((8,)), dma((8,)), dma((8,)), dma((8,)), dma((2,)), dma(()), dma(()),
            dma((4, 8)), dma((4, 8)), dma((4, 2, 2)), dma((2, 2, 2, 2)), dma((2, 2, 2)), dma((2, 2, 2)),
        ],
        compiler_params=pltpu.CompilerParams(
            collective_id=0, has_side_effects=True, vmem_limit_bytes=60 << 20
        ),
        name="layer",
    )(
        queries, span_keys, span_values, prefix_keys, prefix_values, out_weight, residual, block_slot, span_index
    )


def per_device(
    queries, span_keys, span_values, prefix_keys, prefix_values, out_weight, residual, block_slot, span_index
):
    return layer(
        queries[0], span_keys[0], span_values[0], prefix_keys[0], prefix_values[0], out_weight[0], residual[0],
        block_slot, span_index,
    )[None]


def solution(mesh):
    in_specs = (
        P("section", "ctx", "tp"),
        P("section", ("ctx", "tp"), None),
        P("section", ("ctx", "tp"), None),
        P("section", ("ctx", "tp"), None),
        P("section", ("ctx", "tp"), None),
        P("section", "tp", "ctx"),
        P("section", "tp", "ctx"),
        P(),
        P("section"),
    )
    return jax.shard_map(
        per_device, mesh=mesh, in_specs=in_specs, out_specs=P("section", "tp", "ctx"), check_vma=False
    )
```

```python
import functools
import math

import jax
import jax.numpy as jnp
from jax import lax
from jax.experimental import pallas as pl
from jax.experimental.pallas import tpu as pltpu
from jax.sharding import PartitionSpec as P

MESH = pl.DeviceIdType.MESH
HD = 128
BLK = 128
HALF = 64
QB = 1024
PRE = 384
SPN = 64
ROWS = PRE + SPN
SLOT = 2 * ROWS
VR = 144
LOW = -1e30
SLOTS = ((0, 0), (1, 0), (2, 0), (0, 1), (1, 1), (3, 0), (2, 1), (3, 1))
SENT = (1, 2, 3, 4, 6)


def pick(index, table):
    value = jnp.int32(table[-1])
    for position in range(len(table) - 1):
        value = jnp.where(index == position, jnp.int32(table[position]), value)
    return value


def aligned(start, size):
    return pl.ds(pl.multiple_of(start, size), size)


def layer_kernel(
    q_hbm, sk_hbm, sv_hbm, pk_hbm, pv_hbm, w_hbm, res_hbm, slot_ref, limit_ref, out_ref,
    heads, weight, rest, total, part, got, summed, final, stage, kv, q_raw, q_t, k_two, v_t, scores, tri,
    block_max, row_max, acc,
    stage_sem, local_sem, send_sem, recv_sem, fwd_send, fwd_recv, relay_send, q_send, q_recv,
    g_send, g_recv, h_send, h_recv, z_send, z_recv, out_sem,
):
    section, ctx, tp = lax.axis_index("section"), lax.axis_index("ctx"), lax.axis_index("tp")
    x, core = ctx // 2, lax.rem(ctx, 2)
    near = x + 1 - 2 * lax.rem(x, 2)
    chips = (x, near, 3 - x, 3 - near)
    group = x // 2
    odd = lax.rem(section, 2)

    def device(kind, dt=0):
        return (section, chips[kind] * 2 + core, lax.rem(tp + dt, 2))

    sibling = (section, x * 2 + 1 - core, tp)
    twin_section = section + 1 - 2 * odd
    above, below = lax.rem(section + 2, 8), lax.rem(section + 6, 8)

    barrier = pltpu.get_barrier_semaphore()
    greeted = [device(*SLOTS[slot]) for slot in SENT] + [sibling]
    greeted += [(twin_section, ctx, half) for half in range(2)] + [(below, ctx, tp)]
    for other in greeted:
        pl.semaphore_signal(barrier, inc=1, device_id=other, device_id_type=MESH)

    def load_rows(head, dst, sem):
        cols = aligned(head * HD, HD)
        for src, which, at, rows in (
            (pk_hbm, 0, 0, PRE), (pv_hbm, 1, 0, PRE), (sk_hbm, 0, PRE, SPN), (sv_hbm, 1, PRE, SPN)
        ):
            pltpu.make_async_copy(src.at[:, cols], dst.at[which, pl.ds(at, rows)], sem).start()

    blocks = [kv.at[0, core]] + [stage.at[number] for number in range(3)]
    held = ((tp, group), (tp, 1 - group), (1 - tp, group), (1 - tp, 1 - group))
    for number, (side, which) in enumerate(held):
        load_rows(side * 2 + which, blocks[number], stage_sem.at[number])
    own_queries = pltpu.make_async_copy(q_hbm.at[:, aligned(group * 2048, 2048)], q_raw.at[0], local_sem.at[0])
    own_queries.start()

    def wait_block(number):
        pltpu.make_async_copy(blocks[number], blocks[number], stage_sem.at[number]).wait()

    swap = pltpu.make_async_remote_copy(
        src_ref=q_hbm.at[:, aligned((1 - group) * 2048, 2048)], dst_ref=q_raw.at[1], send_sem=q_send,
        recv_sem=q_recv, device_id=device(2), device_id_type=MESH,
    )

    def row_send(slot):
        kind, dt = SLOTS[slot]
        return pltpu.make_async_remote_copy(
            src_ref=blocks[2 * dt + (kind == 2)], dst_ref=kv.at[slot, core], send_sem=send_sem.at[slot],
            recv_sem=recv_sem.at[slot], device_id=device(kind, dt), device_id_type=MESH,
        )

    def relay(slot, to):
        return pltpu.make_async_remote_copy(
            src_ref=kv.at[slot, core], dst_ref=kv.at[to, core], send_sem=relay_send.at[to // 7],
            recv_sem=recv_sem.at[to], device_id=device(1), device_id_type=MESH,
        )

    def to_sibling(slot):
        return pltpu.make_async_remote_copy(
            src_ref=kv.at[slot, core], dst_ref=kv.at[slot, core], send_sem=fwd_send.at[slot],
            recv_sem=fwd_recv.at[slot], device_id=sibling, device_id_type=MESH,
        )

    def arrived_sibling(slot):
        ref = kv.at[slot, 1 - core]
        pltpu.make_async_remote_copy(
            src_ref=ref, dst_ref=ref, send_sem=fwd_send.at[slot], recv_sem=fwd_recv.at[slot],
            device_id=sibling, device_id_type=MESH,
        ).wait_recv()

    def forward(slot):
        pltpu.make_async_copy(kv.at[slot, core], kv.at[slot, core], recv_sem.at[slot]).wait()
        to_sibling(slot).start()

    for number in range(4):
        wait_block(number)
    pl.semaphore_wait(barrier, len(greeted))
    for slot in (2, 1, 6, 3):
        row_send(slot).start()
    to_sibling(0).start()
    load_weight = pltpu.make_async_copy(w_hbm, weight, local_sem.at[1])
    load_rest = pltpu.make_async_copy(res_hbm, rest, local_sem.at[2])
    load_weight.start()
    load_rest.start()

    def source(slot):
        kind = pick(slot, [s[0] for s in SLOTS])
        dt = pick(slot, [s[1] for s in SLOTS])
        chip = jnp.where(kind == 0, x, jnp.where(kind == 1, near, jnp.where(kind == 2, 3 - x, 3 - near)))
        return chip, lax.rem(tp + dt, 2)

    def prepare(slot):
        for c in range(2):
            for start, size, at in ((0, PRE, c * PRE), (PRE, SPN, 2 * PRE + c * SPN)):
                keys = kv[slot, c, 0, pl.ds(start, size)]
                k_two[slot, pl.ds(at, size), :HD] = keys
                k_two[slot, pl.ds(at, size), HD:] = keys
            for page in range(PRE // BLK):
                v_t[slot, :HD, pl.ds(c * PRE + page * BLK, BLK)] = kv[slot, c, 1, pl.ds(page * BLK, BLK)].T
        span_values = jnp.concatenate([kv[slot, c, 1, pl.ds(PRE, SPN)] for c in range(2)], axis=0)
        v_t[slot, :HD, pl.ds(2 * PRE, BLK)] = span_values.T

    def turn_queries(chunk):
        scale = math.log2(math.e) / math.sqrt(HD)

        @pl.loop(0, 8)
        def _(pair):
            for half in range(2):
                rows = pl.ds(half * HALF, HALF)
                block = jnp.concatenate(
                    [q_raw[chunk, rows, aligned((2 * pair + one) * HD, HD)] for one in range(2)], axis=0
                )
                turned = (block.astype(jnp.float32) * scale).T
                high = turned.astype(jnp.bfloat16)
                at = aligned((chunk * 2 + half) * QB + pair * HD, HD)
                q_t[:HD, at] = high
                q_t[HD:, at] = (turned - high.astype(jnp.float32)).astype(jnp.bfloat16)

    ones = jnp.ones((VR - HD, SLOT), jnp.bfloat16)
    for slot in range(8):
        v_t[slot, HD:] = ones
    key_at = lax.broadcasted_iota(jnp.int32, (SPN, QB), 0)
    row_at = lax.rem(lax.broadcasted_iota(jnp.int32, (SPN, QB), 1), HALF)
    tri[0] = jnp.zeros((SPN, QB), jnp.float32)
    tri[1] = jnp.where(key_at <= row_at, 0.0, LOW)
    row_max[...] = jnp.full(row_max.shape, LOW, jnp.float32)

    @pl.loop(0, 4)
    def _(q):
        acc[q] = jnp.zeros((VR, QB), jnp.float32)

    own_queries.wait()
    turn_queries(0)
    arrived_sibling(0)
    prepare(0)

    limit = limit_ref[0] * 8

    def masks(slot, q):
        chip, side = source(slot)
        row_block = jnp.where(q < 2, x, 3 - x) * 4 + core * 2 + lax.rem(q, 2)
        found = []
        for c in range(2):
            for page in range(PRE // BLK):
                number = ((chip * 2 + c) * 2 + side) * (PRE // BLK) + page
                found.append((c * PRE + page * BLK, BLK, slot_ref[number] < limit, None))
        for c in range(2):
            key_block = (chip * 2 + c) * 2 + side
            diagonal = jnp.where(key_block == row_block, 1, 0)
            found.append((2 * PRE + c * SPN, SPN, key_block <= row_block, diagonal))
        return found

    def score(slot, q, buffer):
        value = jnp.dot(k_two[slot], q_t[:, aligned(q * QB, QB)], preferred_element_type=jnp.float32)
        largest = jnp.full((1, QB), LOW, jnp.float32)
        for start, rows, visible, diagonal in masks(slot, q):
            block = value[start : start + rows]
            if diagonal is not None:
                block = block + tri[diagonal]
            scores[buffer, start : start + rows] = block
            largest = jnp.maximum(largest, jnp.where(visible, jnp.max(block, axis=0, keepdims=True), LOW))
        block_max[buffer] = largest

    def process(slot, q, buffer):
        before = row_max[q]
        now = jnp.maximum(before, block_max[buffer])
        row_max[q] = now
        weights = jnp.concatenate(
            [
                jnp.exp2(scores[buffer, start : start + rows] - jnp.where(visible, now, -LOW)).astype(jnp.bfloat16)
                for start, rows, visible, _ in masks(slot, q)
            ],
            axis=0,
        )
        added = jnp.dot(v_t[slot], weights, preferred_element_type=jnp.float32)
        acc[q] = acc[q] * jnp.exp2(before - now) + added

    def place(chip, turn, half, c):
        return heads.at[jnp.where(turn == 0, chip, 3 - chip), chip // 2, half, c]

    def moved(kind, turn, half):
        if kind < 2:
            to = device(kind + 1)
            src, dst = place(x, turn, half, core), place(chips[kind + 1], turn, half, core)
        elif kind < 4:
            to = device(kind - 1)
            rows = pl.ds((kind - 2) * (HALF // 2), HALF // 2)
            src, dst = (place(chip, turn, half, core).at[rows] for chip in (chips[4 - kind], chips[3]))
        else:
            to = sibling
            src, dst = (place(chips[kind - 4], turn, half, c) for c in (core, 1 - core))
        piece = turn * 2 + half
        make = functools.partial(
            pltpu.make_async_remote_copy, send_sem=g_send.at[piece, kind], recv_sem=g_recv.at[piece, kind],
            device_id=to, device_id_type=MESH,
        )
        return make(src_ref=src, dst_ref=src), make(src_ref=dst, dst_ref=dst)

    def send(kind, turn, half):
        moved(kind, turn, half)[0].start()

    def arrived(kind, turn, half):
        moved(kind, turn, half)[1].wait_recv()

    def finish(turn, half):
        q = turn * 2 + half
        share = 1.0 / acc[q, HD : HD + 1]
        mine = place(x, turn, half, core)
        for pair in range(8):
            at = slice(pair * HD, (pair + 1) * HD)
            block = (acc[q, :HD, at] * share[:, at]).T.astype(jnp.bfloat16)
            for one in range(2):
                mine[:, pl.ds((2 * pair + one) * HD, HD)] = block[one * HALF : (one + 1) * HALF]

    def publish(turn, half):
        for kind in (0, 1, 4):
            send(kind, turn, half)

    def pass_on(turn, half):
        arrived(1, turn, half)
        send(2, turn, half)
        send(6, turn, half)
        arrived(0, turn, half)
        send(3, turn, half)
        send(5, turn, half)

    def pass_far(turn, half):
        arrived(2, turn, half)
        arrived(3, turn, half)
        send(7, turn, half)

    def first_part(kind):
        chip = chips[kind]
        for half in range(2):
            arrived(kind + 4, 0, half)
        depth = aligned((chip // 2) * 2048, 2048)

        @pl.loop(0, 2)
        def _(number):
            cols = aligned(number * 512, 512)
            total[chip, :, cols] = jnp.dot(
                heads[chip, chip // 2].reshape(256, 2048), weight[depth, cols], preferred_element_type=jnp.float32
            )

    def hand_on(rows, half, side):
        here = (tp, lax.rem(rows, 2), half, side)
        return pltpu.make_async_remote_copy(
            src_ref=part.at[rows, half, side], dst_ref=got.at[here], send_sem=h_send.at[rows, half, side],
            recv_sem=h_recv.at[here], device_id=(twin_section, ctx, rows // 2), device_id_type=MESH,
        )

    def second_part(kind, half):
        chip = chips[kind]
        rows = 3 - chip
        arrived(kind + 4, 1, half)
        depth = aligned((chip // 2) * 2048, 2048)

        @pl.loop(0, 2)
        def _(number):
            cols = aligned(number * 512, 512)
            value = jnp.dot(
                heads[rows, chip // 2, half].reshape(BLK, 2048), weight[depth, cols],
                preferred_element_type=jnp.float32,
            )
            extra = jnp.concatenate(
                [
                    rest[aligned(lax.rem(rows, 2) * 256 + c * BLK + half * HALF, HALF), cols].astype(jnp.float32)
                    for c in range(2)
                ],
                axis=0,
            )
            value = value + total[rows, pl.ds(half * BLK, BLK), cols] + jnp.where(rows // 2 == tp, extra, 0.0)
            part[rows, half, number] = value.astype(jnp.bfloat16)
            hand_on(rows, half, number).start()

    def climb(unit):
        return pltpu.make_async_remote_copy(
            src_ref=summed.at[unit], dst_ref=final.at[unit], send_sem=z_send.at[unit], recv_sem=z_recv.at[unit],
            device_id=(above, ctx, tp), device_id_type=MESH,
        )

    def collect(which, half):
        @pl.loop(0, 2)
        def _(side):
            unit = (which, half, side)
            for origin in range(2):
                place_of = (origin, *unit)
                ref = got.at[place_of]
                pltpu.make_async_remote_copy(
                    src_ref=ref, dst_ref=ref, send_sem=h_send.at[unit], recv_sem=h_recv.at[place_of],
                    device_id=sibling, device_id_type=MESH,
                ).wait_recv()
            both = got[(0, *unit)].astype(jnp.float32) + got[(1, *unit)].astype(jnp.float32)
            summed[unit] = both.astype(jnp.bfloat16)

            @pl.when(odd == 0)
            def _():
                climb(unit).start()

    def step_at(number):
        slot = jnp.where(number < 16, number // 2, lax.rem(number, 8))
        return slot, jnp.where(number < 16, lax.rem(number, 2), number // 8)

    score(0, 0, 0)

    @pl.loop(0, 8)
    def _(slot):
        for at, slots in ((2, (3,)), (3, (6, 4)), (4, (5,)), (6, (7,))):

            @pl.when(slot == at)
            def _():
                for which in slots:
                    forward(which)
                    if which == 6:
                        relay(6, 7).start()

        score(slot, 1, 1)
        process(slot, 0, 0)

        @pl.when(slot == 0)
        def _():
            forward(1)
            forward(2)
            relay(2, 5).start()
            row_send(4).start()
            swap.start()

        @pl.when(slot < 7)
        def _():
            arrived_sibling(slot + 1)
            prepare(slot + 1)
            score(slot + 1, 0, 0)
            process(slot, 1, 1)

        @pl.when(slot == 7)
        def _():
            finish(0, 0)
            publish(0, 0)
            process(slot, 1, 1)

    finish(0, 1)
    publish(0, 1)
    swap.wait_recv()
    turn_queries(1)
    score(0, 2, 0)

    @pl.loop(8, 16)
    def _(turn):
        @pl.when(turn == 12)
        def _():
            pass_on(0, 0)

        @pl.when(turn == 13)
        def _():
            pass_on(0, 1)

        @pl.when(turn == 14)
        def _():
            first_part(2)
            second_part(0, 0)

        score(*step_at(2 * turn + 1), 1)
        process(*step_at(2 * turn), 0)
        score(*step_at(jnp.minimum(2 * turn + 2, 31)), 0)
        process(*step_at(2 * turn + 1), 1)

        @pl.when(turn == 11)
        def _():
            finish(1, 0)
            publish(1, 0)

        @pl.when(turn == 10)
        def _():
            load_weight.wait()
            load_rest.wait()

    finish(1, 1)
    for half in range(2):
        pass_far(0, half)
    first_part(0)
    pass_on(1, 0)
    publish(1, 1)
    second_part(2, 0)
    first_part(3)
    second_part(1, 0)
    first_part(1)
    pass_far(1, 0)
    second_part(3, 0)
    second_part(0, 1)
    early = jnp.where(tp == (3 - x) // 2, lax.rem(3 - x, 2), lax.rem(x, 2))
    collect(early, 0)
    pass_on(1, 1)
    second_part(2, 1)
    second_part(1, 1)
    collect(1 - early, 0)
    pass_far(1, 1)
    second_part(3, 1)
    collect(early, 1)
    collect(1 - early, 1)

    def write(ref, unit):
        which, half, side = unit
        copies = []
        for c in range(2):
            rows = aligned(which * 256 + c * BLK + half * HALF, HALF)
            copies.append(
                pltpu.make_async_copy(
                    ref.at[(*unit, pl.ds(c * HALF, HALF))], out_ref.at[rows, aligned(side * 512, 512)],
                    out_sem.at[(*unit, c)],
                )
            )
        return copies

    def unit_of(number):
        return (lax.rem(number // 2, 2), number // 4, lax.rem(number, 2))

    @pl.loop(0, 8)
    def _(number):
        unit = unit_of(number)

        @pl.when(odd == 0)
        def _():
            climb(unit).wait_recv()
            for copy in write(final, unit):
                copy.start()

        @pl.when(odd == 1)
        def _():
            for copy in write(summed, unit):
                copy.start()

    @pl.loop(0, 8)
    def _(number):
        for copy in write(final, unit_of(number)):
            copy.wait()

    for slot in SENT:
        row_send(slot).wait_send()
    relay(2, 5).wait_send()
    relay(6, 7).wait_send()
    swap.wait_send()

    @pl.loop(0, 8)
    def _(slot):
        to_sibling(slot).wait_send()

    @pl.loop(0, 4)
    def _(piece):
        for kind in range(8):
            moved(kind, piece // 2, lax.rem(piece, 2))[0].wait_send()

        for half in range(2):
            for side in range(2):
                hand_on(piece, half, side).wait_send()

        @pl.when(odd == 0)
        def _():
            for side in range(2):
                climb((piece // 2, lax.rem(piece, 2), side)).wait_send()


def layer(
    queries, span_keys, span_values, prefix_keys, prefix_values, out_weight, residual, block_slot, span_index
):
    any_spec = pl.BlockSpec(memory_space=pl.ANY)
    smem = pl.BlockSpec(memory_space=pltpu.SMEM)
    dma = pltpu.SemaphoreType.DMA
    bf16, f32 = jnp.bfloat16, jnp.float32
    return pl.pallas_call(
        layer_kernel,
        out_shape=jax.ShapeDtypeStruct((512, 1024), bf16),
        in_specs=[any_spec] * 7 + [smem, smem],
        out_specs=any_spec,
        scratch_shapes=[
            pltpu.VMEM((4, 2, 2, 2, HALF, 2048), bf16),
            pltpu.VMEM((4096, 1024), bf16),
            pltpu.VMEM((512, 1024), bf16),
            pltpu.VMEM((4, 256, 1024), f32),
            pltpu.VMEM((4, 2, 2, BLK, 512), bf16),
            pltpu.VMEM((2, 2, 2, 2, BLK, 512), bf16),
            pltpu.VMEM((2, 2, 2, BLK, 512), bf16),
            pltpu.VMEM((2, 2, 2, BLK, 512), bf16),
            pltpu.VMEM((3, 2, ROWS, HD), bf16),
            pltpu.VMEM((8, 2, 2, ROWS, HD), bf16),
            pltpu.VMEM((2, BLK, 2048), bf16),
            pltpu.VMEM((2 * HD, 4 * QB), bf16),
            pltpu.VMEM((8, SLOT, 2 * HD), bf16),
            pltpu.VMEM((8, VR, SLOT), bf16),
            pltpu.VMEM((2, SLOT, QB), f32),
            pltpu.VMEM((2, SPN, QB), f32),
            pltpu.VMEM((2, 1, QB), f32),
            pltpu.VMEM((4, 1, QB), f32),
            pltpu.VMEM((4, VR, QB), f32),
            dma((4,)), dma((3,)), dma((8,)), dma((8,)), dma((8,)), dma((8,)), dma((2,)), dma(()), dma(()),
            dma((4, 8)), dma((4, 8)), dma((4, 2, 2)), dma((2, 2, 2, 2)), dma((2, 2, 2)), dma((2, 2, 2)),
            dma((2, 2, 2, 2)),
        ],
        compiler_params=pltpu.CompilerParams(
            collective_id=0, has_side_effects=True, vmem_limit_bytes=60 << 20
        ),
        name="layer",
    )(
        queries, span_keys, span_values, prefix_keys, prefix_values, out_weight, residual, block_slot, span_index
    )


def per_device(
    queries, span_keys, span_values, prefix_keys, prefix_values, out_weight, residual, block_slot, span_index
):
    return layer(
        queries[0], span_keys[0], span_values[0], prefix_keys[0], prefix_values[0], out_weight[0], residual[0],
        block_slot, span_index,
    )[None]


def solution(mesh):
    in_specs = (
        P("section", "ctx", "tp"),
        P("section", ("ctx", "tp"), None),
        P("section", ("ctx", "tp"), None),
        P("section", ("ctx", "tp"), None),
        P("section", ("ctx", "tp"), None),
        P("section", "tp", "ctx"),
        P("section", "tp", "ctx"),
        P(),
        P("section"),
    )
    return jax.shard_map(
        per_device, mesh=mesh, in_specs=in_specs, out_specs=P("section", "tp", "ctx"), check_vma=False
    )
```
